256 devices in a mesh: region: 32 (over y, x, core), replica: 8 (over z).
Axes of the slice: x: 4, y: 4, z: 8, core: 2. Of those that a mesh axis runs over, the one named last changes fastest.
Arguments:
- positions: float32 [3, 16384, 64], P(None, ('region', 'replica')), may hold values from -1 to 1
- spacing: bfloat16 [16384, 64], P(('region', 'replica')), may hold values from 0.0049743652 to 0.059814453
- targets: float32 [3, 16384], P(None, ('region', 'replica')), may hold values from 0 to 1
- seg_region: int32 [16384, 4, 1], P(('region', 'replica')), may hold values from 0 to 63; in each aligned block of 256 rows (0 to 255, 256 to 511, ..., all dimensions but the last counted through in order) at most 12 rows name the same one
- seg_rank: int32 [16384, 4], P(('region', 'replica')), may hold values from 0 to 3, each once within a row
- frequencies: float32 [3, 128], replicated, may hold values from -6 to 6
- w_in: float32 [64, 256, 256], P('region'), may hold values from -0.375 to 0.375
- w_mid: float32 [64, 256, 256], P('region'), may hold values from -0.375 to 0.375
- w_out: float32 [64, 4, 256], P('region'), may hold values from -0.375 to 0.375
Outputs:
- colour: float32 [3, 16384], P(None, ('region', 'replica'))
- grad_in: float32 [64, 256, 256], P('region')
- grad_mid: float32 [64, 256, 256], P('region')
- grad_out: float32 [64, 4, 256], P('region')
The draws below stay inside these ranges and needn't reach their ends.
Inputs may be any that keep to these rules, and one draw needn't show every extreme that they name: `seg_region`: among the 256 segments of the rays of one device no region is named more than 12 times. `seg_rank`: each ray's row is a permutation.
All inputs are finite; a program needn't handle non-finite values.
Results may differ from the reference program's by a relative error of at most 0.014.
The reference program's roundings to bfloat16 on the way count: a program that leaves them out, or rounds other values in their place, can miss the bound.
Values may be sent and summed in bfloat16 or wider, within the bound.
A program may use at most 128 MiB of HBM per device.

```python
import math
import jax
import jax.numpy as jnp
import numpy as np
from jax import lax

RAY_DEV = 64
SEGS = 4
SEG_LEN = 16
FREQ = 128
HID = 256
REGIONS = 64
ENC = 256
SAMPLES = 64
CAP = 12
RAYS = 16384
N_REGION = 32
N_REPLICA = 8


def block_levels(key, extent, cuts, low, high):
    def one(dim, blocks):
        draws = jax.random.uniform(jax.random.fold_in(jax.random.fold_in(key, 6), dim), (blocks,), jnp.float32, low / len(cuts), high / len(cuts))
        return jnp.repeat(jnp.exp(draws), extent[dim] // blocks).reshape((-1,) + (1,) * (len(extent) - dim - 1))

    gain = one(*cuts[0])
    for cut in cuts[1:]:
        gain = gain * one(*cut)
    return gain


def deal_out(own_key, own, number, rows, amount, top, bound, slope):
    sequence = jax.random.permutation(own_key, amount)
    crowded, usual = portions_of(amount, rows * top, bound, slope, True), portions_of(amount, rows * top, bound, slope, False)
    places = jnp.arange(amount)

    def named(sizes, rotation):
        used = int((sizes > 0).sum())
        fixed = max(1, used // 4)
        moved = fixed + (places - fixed + rotation * (used - fixed)) % max(1, amount - fixed)
        return jnp.zeros((amount,), jnp.int32).at[sequence[jnp.where(places < fixed, places, moved)]].set(jnp.asarray(sizes, jnp.int32))

    sizes = jnp.where(number % 4 == 0, named(crowded, number // 4), named(usual, number - number // 4 - 1))
    mixed = jax.random.permutation(jax.random.fold_in(own, 3), amount)
    giver, taker = mixed[0:amount // 2 * 2:2], mixed[1:amount // 2 * 2:2]
    margin = jnp.minimum(sizes[giver] - 1, bound - sizes[taker]) // 2
    margin = jnp.where((giver == sequence[0]) | (taker == sequence[0]) | (sizes[taker] == 0), 0, jnp.maximum(margin, 0))
    moved = jax.random.randint(jax.random.fold_in(own, 4), (amount // 2,), 0, 1 << 20) % (margin + 1)
    sizes = sizes.at[giver].add(-moved).at[taker].add(moved)
    items = jnp.searchsorted(jnp.cumsum(sizes), jnp.arange(rows * top), side="right").astype(jnp.int32)
    table = items.reshape(top, rows).T
    table = table[jax.random.permutation(jax.random.fold_in(own, 1), rows)]
    rotation = jax.random.randint(jax.random.fold_in(own, 2), (rows, 1), 0, top)
    return jnp.take_along_axis(table, (jnp.arange(top)[None, :] + rotation) % top, axis=1)


def portions_of(number_of, total, limit, slope, full):
    weights = [(1 << 20) // math.isqrt(rank ** slope) + 1 for rank in range(1, number_of + 1)]
    largest = limit if full else min(limit, max(-(-total // number_of), total * weights[0] // sum(weights)))
    least = 1 if total - largest >= number_of - 1 else 0
    given, spare = [largest] + [least] * (number_of - 1), total - largest - least * (number_of - 1)
    while spare > 0:
        free = [i for i in range(1, number_of) if given[i] < largest] or [i for i in range(1, number_of) if given[i] < limit]
        pool, left = sum([weights[i] for i in free]), spare
        for i in free:
            extra = min(limit - given[i], max(1, left * weights[i] // pool), spare)
            given[i] = given[i] + extra
            spare = spare - extra
    return np.array(given)


def gaussian(own_key, extent, width, bound, cuts=(), kind=jnp.bfloat16):
    values = jax.random.normal(own_key, extent, jnp.float32) * width
    if len(cuts) > 0:
        values = block_levels(own_key, extent, cuts, -0.22, 0.18) * values
    return jnp.clip(values, min=-bound, max=bound).astype(kind)


def setup_inputs(seed: int = 0) -> dict:
    key_of = jax.random.split(jax.random.key(seed), 10)
    positions = jnp.clip(jax.random.uniform(key_of[0], (3, RAYS, SAMPLES), jnp.float32, -1.0, 1.0) * block_levels(key_of[0], (3, RAYS, SAMPLES), ((1, 256),), -0.4, 0.0), -1.0, 1.0)
    spacing = jnp.clip(jnp.exp(math.log(0.059814453) - 2.48694955 * jax.random.uniform(key_of[1], (RAYS, SAMPLES), jnp.float32) ** block_levels(key_of[1], (RAYS, SAMPLES), ((0, 256),), -0.2, 0.2)), 0.0049743652, 0.059814453).astype(jnp.bfloat16)
    targets = jnp.clip(1.0 * jax.random.uniform(key_of[2], (3, RAYS), jnp.float32) ** block_levels(key_of[2], (3, RAYS), ((1, 256),), -0.2, 0.2), 0.0, 1.0)
    seg_region_keys = jax.random.split(jax.random.fold_in(key_of[3], 1), RAYS * SEGS // (RAY_DEV * SEGS))
    seg_region_turns = jax.random.permutation(jax.random.fold_in(key_of[3], 3), RAYS * SEGS // (RAY_DEV * SEGS))
    seg_region = jax.vmap(lambda own, number: deal_out(jax.random.fold_in(key_of[3], 2), own, number, RAY_DEV * SEGS, REGIONS, 1, CAP, 2))(seg_region_keys, seg_region_turns).reshape((RAYS, SEGS, 1))
    seg_rank = jax.vmap(lambda own: jax.random.permutation(own, SEGS))(jax.random.split(key_of[4], RAYS)).reshape((RAYS, SEGS)).astype(jnp.int32)
    frequencies = gaussian(key_of[5], (3, FREQ), 1.5, 6.0, (), jnp.float32)
    w_in = gaussian(key_of[6], (REGIONS, ENC, HID), ENC ** -0.5, 0.375, ((0, 32),), jnp.float32)
    w_mid = gaussian(key_of[7], (REGIONS, HID, HID), HID ** -0.5, 0.375, ((0, 32),), jnp.float32)
    w_out = gaussian(key_of[8], (REGIONS, 4, HID), HID ** -0.5, 0.375, ((0, 32),), jnp.float32)
    return dict(positions=positions, spacing=spacing, targets=targets, seg_region=seg_region, seg_rank=seg_rank, frequencies=frequencies, w_in=w_in, w_mid=w_mid, w_out=w_out)


two_pi = 2.0 * math.pi
loss_scale = 16.0

def encode(coords, frequencies):
    phases = coords[..., 0, :, None] * frequencies[0] + coords[..., 1, :, None] * frequencies[1] + coords[..., 2, :, None] * frequencies[2]
    phases = two_pi * phases
    return jnp.concatenate([jnp.sin(phases), jnp.cos(phases)], -1).astype(jnp.bfloat16)

def mlp_forward(features, layer_in, layer_mid, layer_out):
    hidden_one = jax.nn.relu(jnp.dot(features, layer_in, preferred_element_type=jnp.float32)).astype(jnp.bfloat16)
    hidden_two = jax.nn.relu(jnp.dot(hidden_one, layer_mid, preferred_element_type=jnp.float32)).astype(jnp.bfloat16)
    raw_out = jnp.dot(layer_out, hidden_two.T, preferred_element_type=jnp.float32)
    return (hidden_one, hidden_two, raw_out)

def mlp_backward(features, hidden_one, hidden_two, raw_grad, layer_mid, layer_out):
    grad_out = jnp.dot(raw_grad, hidden_two.astype(jnp.float32), precision=lax.Precision.HIGHEST)
    grad_two = (jnp.dot(raw_grad.T, layer_out.astype(jnp.float32), precision=lax.Precision.HIGHEST) * (hidden_two > 0)).astype(jnp.bfloat16)
    grad_mid = jnp.dot(hidden_one.T, grad_two, preferred_element_type=jnp.float32)
    grad_one = (jnp.dot(grad_two, layer_mid.T, preferred_element_type=jnp.float32) * (hidden_one > 0)).astype(jnp.bfloat16)
    grad_in = jnp.dot(features.T, grad_one, preferred_element_type=jnp.float32)
    return (grad_in, grad_mid, grad_out)

def render(raw_out, gap_rows):
    density = jax.nn.softplus(raw_out[0])
    emitted = jax.nn.sigmoid(raw_out[1:])
    optical = density * gap_rows.astype(jnp.float32)
    cumulative = jnp.cumsum(optical, axis=-1)
    weight = jnp.exp(-(cumulative - optical)) - jnp.exp(-cumulative)
    seg_colour = lax.optimization_barrier(jnp.sum(weight * emitted, axis=-1))
    transmit = jnp.exp(-cumulative[..., -1])
    return jnp.concatenate([seg_colour, transmit[None]], 0)

def composite(seg_colour, seg_trans, seg_rank):
    before = seg_rank[:, None, :] < seg_rank[:, :, None]
    factor = jnp.where(before, seg_trans[:, None, :], jnp.ones_like(seg_trans)[:, None, :])
    prefix = jnp.prod(factor, axis=-1)
    return lax.optimization_barrier(jnp.sum(seg_colour * prefix[None], axis=-1))

def reference(positions, spacing, targets, seg_region, seg_rank, frequencies, w_in, w_mid, w_out):
    count_all = RAYS * SEGS
    seg_pos = positions.reshape(3, count_all, SEG_LEN).transpose(1, 0, 2)
    seg_gap = spacing.reshape(count_all, SEG_LEN)
    region_of = seg_region.reshape(count_all).astype(jnp.int32)
    ranked = jnp.argsort(region_of, stable=True).astype(jnp.int32)
    counts = lax.optimization_barrier(jnp.sum((region_of[None, :] == jnp.arange(REGIONS, dtype=jnp.int32)[:, None]).astype(jnp.int32), axis=1))
    starts = (jnp.cumsum(counts) - counts).astype(jnp.int32)
    widest = N_REGION * N_REPLICA * CAP
    ranked_pad = jnp.concatenate([ranked, jnp.zeros((widest,), jnp.int32)])
    slot_range = jnp.arange(widest, dtype=jnp.int32)
    member_ids = jax.vmap(lambda begin: lax.dynamic_slice(ranked_pad, (begin,), (widest,)))(starts)
    in_use = slot_range[None, :] < counts[:, None]
    region_ids = jnp.arange(REGIONS, dtype=jnp.int32)

    def prepare(operands):
        region_id, ids_here, use_here = operands
        gap_rows = seg_gap[ids_here]
        gap_rows = jnp.where(use_here[:, None], gap_rows, jnp.zeros_like(gap_rows))
        features = encode(seg_pos[ids_here], frequencies).reshape(widest * SEG_LEN, ENC)
        layer_in = w_in[region_id].astype(jnp.bfloat16)
        layer_mid = w_mid[region_id].astype(jnp.bfloat16)
        layer_out = w_out[region_id].astype(jnp.bfloat16)
        return (gap_rows, features, layer_in, layer_mid, layer_out)

    def forward_region(operands):
        gap_rows, features, layer_in, layer_mid, layer_out = prepare(operands)
        raw_out = mlp_forward(features, layer_in, layer_mid, layer_out)[2]
        rendered = render(raw_out.reshape(4, widest, SEG_LEN), gap_rows)
        rendered = jnp.where(operands[2][None, :], rendered, jnp.zeros_like(rendered))
        return rendered.T
    pieces = lax.map(forward_region, (region_ids, member_ids, in_use))
    seg_out = jnp.zeros((count_all, 4), jnp.float32).at[member_ids.reshape(-1)].add(pieces.reshape(-1, 4))
    seg_colour = seg_out[:, :3].T.reshape(3, RAYS, SEGS)
    seg_trans = seg_out[:, 3].reshape(RAYS, SEGS)
    colour, pullback = jax.vjp(lambda col, tra: composite(col, tra, seg_rank), seg_colour, seg_trans)
    colour_grad = 2.0 * loss_scale * (colour - targets)
    seg_colour_grad, seg_trans_grad = pullback(colour_grad)
    seg_cot = jnp.concatenate([seg_colour_grad.reshape(3, count_all).T, seg_trans_grad.reshape(count_all, 1)], 1)

    def backward_region(operands):
        gap_rows, features, layer_in, layer_mid, layer_out = prepare(operands)
        cotangent = seg_cot[operands[1]]
        cotangent = jnp.where(operands[2][:, None], cotangent, jnp.zeros_like(cotangent)).T
        hidden_one, hidden_two, raw_out = mlp_forward(features, layer_in, layer_mid, layer_out)
        raw_four = raw_out.reshape(4, widest, SEG_LEN)
        render_pull = jax.vjp(lambda values: render(values, gap_rows), raw_four)[1]
        raw_grad = render_pull(cotangent)[0].reshape(4, widest * SEG_LEN)
        return mlp_backward(features, hidden_one, hidden_two, raw_grad, layer_mid, layer_out)
    grad_in, grad_mid, grad_out = lax.map(backward_region, (region_ids, member_ids, in_use))
    return (colour, grad_in, grad_mid, grad_out)
```

```python
import functools
import math

import jax
import jax.numpy as jnp
from jax import lax
from jax.experimental import pallas as pl
from jax.experimental.pallas import tpu as pltpu
from jax.sharding import PartitionSpec as P

MESH = pl.DeviceIdType.MESH
f32, bf16 = jnp.float32, jnp.bfloat16
LANES = 128
ROW = 32
GROUP = LANES // ROW
loss_scale = 16.0

SIN_HALF = (4.442882919048677, -7.308245676836255, 3.606354025126868, -0.8461104138552027, 0.10982204430121903)
COS_HALF = (1.4142134959439656, -6.978850908781684, 5.739459581977078, -1.8835528214703008, 0.31067786282805515)


def iota(shape, dim):
    return lax.broadcasted_iota(jnp.int32, shape, dim)


def dot(a, b):
    return jnp.dot(a, b, preferred_element_type=f32)


def dot_nt(a, b):
    return lax.dot_general(a, b, (((1,), (1,)), ((), ())), preferred_element_type=f32)


def dot_tn(a, b):
    return lax.dot_general(a, b, (((0,), (0,)), ((), ())), preferred_element_type=f32)


def split(x):
    high = x.astype(bf16).astype(f32)
    rest = x - high
    middle = rest.astype(bf16).astype(f32)
    return high, middle, rest - middle


def wide(x):
    return jnp.concatenate(split(x), 1).astype(bf16)


def tall(x):
    return jnp.concatenate((*split(x), jnp.zeros_like(x)), 0).astype(bf16)


def unwide(x):
    w = x.shape[1] // 3
    return x[:, :w] + x[:, w : 2 * w] + x[:, 2 * w :]


def untall(x):
    w = x.shape[0] // 4
    return x[:w] + x[w : 2 * w] + x[2 * w : 3 * w]


def polynomial(coefficients, z):
    value = jnp.full_like(z, coefficients[-1])
    for coefficient in coefficients[-2::-1]:
        value = value * z + coefficient
    return value


def sin_cos_turns(turns):
    rest = turns - jnp.round(turns)
    square = rest * rest
    s = polynomial(SIN_HALF, square) * rest
    c = polynomial(COS_HALF, square)
    return s * c, 1.0 - s * s


def column_of(x, index):
    return jnp.sum(jnp.where(iota(x.shape, 1) == index, x, 0.0), axis=1, keepdims=True)


def on_lanes(x, width=LANES):
    return jnp.concatenate([x, jnp.zeros((x.shape[0], width - x.shape[1]), x.dtype)], 1)


def exchange_start(count, me, axis, source_of, target, send, recv):
    def start(k, carry):
        peer = lax.rem(me + k, count)
        pltpu.make_async_remote_copy(
            src_ref=source_of(peer),
            dst_ref=target.at[me],
            send_sem=send.at[k],
            recv_sem=recv.at[k],
            device_id={axis: peer},
            device_id_type=MESH,
        ).start()
        return carry

    lax.fori_loop(1, count, start, 0)


def exchange_wait(count, me, axis, source_of, target, send, recv):
    def wait(k, carry):
        peer = lax.rem(me + k, count)
        origin = lax.rem(me + count - k, count)
        pltpu.make_async_remote_copy(
            src_ref=source_of(peer),
            dst_ref=target.at[origin],
            send_sem=send.at[k],
            recv_sem=recv.at[k],
            device_id={axis: peer},
            device_id_type=MESH,
        ).wait()
        return carry

    lax.fori_loop(1, count, wait, 0)


def step_kernel(
    n, m, cap, segs, seg_len,
    pos_ref, gap_ref, tgt_ref, reg_ref, rank_ref, freq_ref, w_in_ref, w_mid_ref, w_out_ref,
    colour_ref, grads_ref, grad_out_ref,
    send_a, recv_a, send_b, recv_b, send_c, recv_c,
    feat, hid_one, hid_two, raw, shade, alpha, gaps, cot, raw_grad,
    place, phase_hi, phase_lo, slots_x, wb_in, wb_mid, wb_out,
    acc_in, acc_mid, acc_out, part, part_recv, out_send, out_recv,
    sem_a, sem_b, sem_c, sem_rs, sem_ag, sem_go,
):
    me = lax.axis_index("region")
    mez = lax.axis_index("replica")
    owned = w_in_ref.shape[0]
    rays = pos_ref.shape[1]
    seg_dev = rays * segs
    taken = owned * cap
    slots = n * cap
    chunks = seg_len // 2
    rows = recv_a.shape[1]

    barrier = pltpu.get_barrier_semaphore()

    def greet_region(k, carry):
        pl.semaphore_signal(
            barrier, inc=1, device_id={"region": lax.rem(me + k, n)}, device_id_type=MESH
        )
        return carry

    def greet_replica(k, carry):
        pl.semaphore_signal(
            barrier, inc=1, device_id={"replica": lax.rem(mez + k, m)}, device_id_type=MESH
        )
        return carry

    lax.fori_loop(1, n, greet_region, 0)
    lax.fori_loop(1, m, greet_replica, 0)

    regions = reg_ref[...].astype(f32)
    region_col = jnp.concatenate([column_of(regions, s) for s in range(segs)], 0)
    lane = iota((seg_dev, LANES), 1)
    lane_f = lane.astype(f32)
    onehot = jnp.where(region_col == lane_f, 1.0, 0.0)
    before = jnp.where(iota((seg_dev, seg_dev), 0) > iota((seg_dev, seg_dev), 1), 1.0, 0.0)
    earlier = dot(before.astype(bf16), onehot.astype(bf16))
    order_col = jnp.sum(earlier * onehot, axis=1, keepdims=True)
    owner_col = jnp.floor((region_col + 0.5) * (1.0 / owned))
    unit_col = (region_col - owned * owner_col) * cap + order_col
    slot_col = owner_col * rows + unit_col
    keys = jnp.where(lane == 0, slot_col, jnp.where(lane == 1, owner_col, 0.0)).T
    slot_row, owner_row = keys[0:1, :], keys[1:2, :]

    pieces = []
    for s in range(segs):
        lane_s = iota((rays, LANES), 1)
        packed = jnp.zeros((rays, LANES), f32)
        for d in range(3):
            moved = pltpu.roll(on_lanes(pos_ref[d]), (seg_len * (d - s)) % LANES, 1)
            packed = jnp.where((lane_s >= seg_len * d) & (lane_s < seg_len * (d + 1)), moved, packed)
        moved = pltpu.roll(on_lanes(gap_ref[...].astype(f32)), (seg_len * (3 - s)) % LANES, 1)
        packed = jnp.where((lane_s >= seg_len * 3) & (lane_s < seg_len * 4), moved, packed)
        pieces.append(packed)
    packed = wide(jnp.concatenate(pieces, 0))
    scatter = jnp.where(iota((n * rows, seg_dev), 0).astype(f32) == slot_row, 1.0, 0.0).astype(bf16)
    send_a[...] = unwide(dot(scatter, packed)).reshape(send_a.shape)

    pl.semaphore_wait(barrier, n - 1 + m - 1)
    exchange_a = (n, me, "region", lambda p: send_a.at[p], recv_a, sem_a.at[0], sem_a.at[1])
    exchange_start(*exchange_a)
    recv_a[me] = send_a[me]

    for l in range(owned):
        wb_in[l] = w_in_ref[l].astype(bf16)
        wb_mid[l] = w_mid_ref[l].astype(bf16)
        wb_out[l] = jnp.concatenate([w_out_ref[l], jnp.zeros((4, w_out_ref.shape[2]), f32)], 0).astype(bf16)
        slot_id = iota((slots, 1), 0).astype(f32)
        peer_id = jnp.floor((slot_id + 0.5) * (1.0 / cap))
        spot = slot_id + (ROW - cap) * peer_id + l * cap
        place[l] = jnp.where(iota((slots, n * ROW), 1).astype(f32) == spot, 1.0, 0.0).astype(bf16)
    freq_high, freq_middle, freq_low = split(freq_ref[...])
    width = freq_ref.shape[1]

    def spread(values):
        return jnp.concatenate([jnp.broadcast_to(values[d : d + 1], (seg_len, width)) for d in range(3)], 0)

    rest16 = jnp.zeros((seg_len, width), f32)
    rest32 = jnp.zeros((2 * seg_len, width), f32)
    table_hi = jnp.concatenate(
        [spread(freq_high), spread(freq_high), rest32, spread(freq_high), rest16, spread(freq_middle), rest16], 0
    )
    table_lo = jnp.concatenate([spread(freq_low), spread(freq_middle), rest32], 0)
    for i in range(seg_len):
        cols = slice((i % 2) * width, (i % 2 + 1) * width)
        mine = (iota(table_hi.shape, 0) & (seg_len - 1)) == i
        phase_hi[i // 2, :, cols] = jnp.where(mine, table_hi, 0.0).astype(bf16)
        mine = (iota(table_lo.shape, 0) & (seg_len - 1)) == i
        phase_lo[i // 2, :, cols] = jnp.where(mine, table_lo, 0.0).astype(bf16)

    exchange_wait(*exchange_a)

    pad = jnp.zeros((n, ROW - rows, LANES), f32)
    received = jnp.concatenate([recv_a[...], pad], 1).reshape(n * ROW, LANES)
    high, middle, low = split(received)
    lane = iota(received.shape, 1)
    coords = 3 * seg_len
    first = jnp.where(lane < coords, high, pltpu.roll(middle, coords, 1))
    second = jnp.where(lane < coords, low, jnp.where(lane < LANES // 2, high, pltpu.roll(high, LANES // 2, 1)))
    received = jnp.concatenate([first, second], 1).astype(bf16)
    pick_gap = jnp.where(
        iota((seg_len, 2 * LANES), 1) == iota((seg_len, 2 * LANES), 0) + LANES + coords, 1.0, 0.0
    ).astype(bf16)
    for l in range(owned):
        slots_x[l] = dot(place[l], received).astype(bf16)
        gaps[l] = dot_nt(pick_gap, slots_x[l])

    sub = iota((8, slots), 0)
    returned = jnp.zeros((8, n * ROW), f32)
    for l in range(owned):

        def forward(c, carry):
            turns = dot(slots_x[l], phase_hi[c]) + dot(slots_x[l][:, :LANES], phase_lo[c])
            sines, cosines = sin_cos_turns(turns)
            for j in range(2):
                cols = slice(j * width, (j + 1) * width)
                feat[l, c, j * slots : (j + 1) * slots, :] = jnp.concatenate(
                    [sines[:, cols], cosines[:, cols]], 1
                ).astype(bf16)
            one = jnp.maximum(dot(feat[l, c], wb_in[l]), 0.0).astype(bf16)
            hid_one[l, c] = one
            two = jnp.maximum(dot(one, wb_mid[l]), 0.0).astype(bf16)
            hid_two[l, c] = two
            raw[c] = dot_nt(wb_out[l], two)
            return carry

        lax.fori_loop(0, chunks, forward, 0)

        depth = jnp.zeros((8, slots), f32)
        clear = jnp.ones((8, slots), f32)
        colour = jnp.zeros((8, slots), f32)
        for i in range(seg_len):
            value = raw[i // 2][:, (i % 2) * slots : (i % 2 + 1) * slots]
            density = jnp.broadcast_to(value[0:1], value.shape)
            density = jnp.maximum(density, 0.0) + jnp.log1p(jnp.exp(-jnp.abs(density)))
            emitted = 1.0 / (1.0 + jnp.exp(-value))
            depth = depth + density * gaps[l][i : i + 1]
            after = jnp.exp(-depth)
            colour = colour + (clear - after) * emitted
            clear = after
            shade[l, i] = emitted
            alpha[l, i] = after
        rendered = jnp.where(sub == 0, clear, colour)
        returned = returned + untall(dot(tall(rendered), place[l]))
    for q in range(send_b.shape[0]):
        send_b[q] = returned[:, q * LANES : (q + 1) * LANES]

    exchange_b = (n, me, "region", lambda p: send_b.at[p // GROUP], recv_b, sem_b.at[0], sem_b.at[1])
    exchange_start(*exchange_b)
    recv_b[me] = send_b[me // GROUP]

    lane = iota((seg_dev, LANES), 1)
    unit_mask = (lane & (ROW - 1)).astype(f32) == unit_col
    owner_mask = jnp.where(iota((seg_dev, n), 1).astype(f32) == owner_col, 1.0, 0.0).astype(bf16)
    owner_turned = jnp.where(iota((n, seg_dev), 0).astype(f32) == owner_row, 1.0, 0.0).astype(bf16)
    ranks = rank_ref[...].astype(f32)
    rank = [column_of(ranks, s) for s in range(segs)]
    earlier_than = [[rank[t] < rank[s] for t in range(segs)] for s in range(segs)]
    eye = iota((rays, rays), 0) == iota((rays, rays), 1)
    target = [
        jnp.sum(jnp.where(eye, tgt_ref[c : c + 1, :], 0.0), axis=1, keepdims=True) for c in range(3)
    ]
    shift_home = lax.rem(me, GROUP) * ROW

    exchange_wait(*exchange_b)

    lane_n = iota((n, LANES), 1)
    mine = jnp.zeros((n, LANES), f32)
    for ch in range(4):
        moved = pltpu.roll(recv_b[:, ch, :], lax.rem(ch * ROW - shift_home + LANES, LANES), 1)
        mine = jnp.where((lane_n >= ch * ROW) & (lane_n < (ch + 1) * ROW), moved, mine)
    found = jnp.where(unit_mask, unwide(dot(owner_mask, wide(mine))), 0.0)
    columns = [
        jnp.sum(jnp.where((lane >= ch * ROW) & (lane < (ch + 1) * ROW), found, 0.0), axis=1, keepdims=True)
        for ch in range(4)
    ]
    by_seg = [[col[s * rays : (s + 1) * rays] for s in range(segs)] for col in columns]
    trans, colours = by_seg[0], by_seg[1:]

    def front(s, skip):
        product = jnp.ones((rays, 1), f32)
        for t in range(segs):
            if t not in skip:
                product = product * jnp.where(earlier_than[s][t], trans[t], 1.0)
        return product

    prefix = [front(s, (s,)) for s in range(segs)]
    pulled = []
    for c in range(3):
        total = colours[c][0] * prefix[0]
        for s in range(1, segs):
            total = total + colours[c][s] * prefix[s]
        colour_ref[c : c + 1, :] = jnp.sum(
            jnp.where(eye, jnp.broadcast_to(total, eye.shape), 0.0), axis=0, keepdims=True
        )
        pulled.append((2.0 * loss_scale) * (total - target[c]))
    weight = [
        pulled[0] * colours[0][s] + pulled[1] * colours[1][s] + pulled[2] * colours[2][s] for s in range(segs)
    ]
    back = [[], [], [], []]
    for t in range(segs):
        total = jnp.zeros((rays, 1), f32)
        for s in range(segs):
            if s != t:
                total = total + jnp.where(earlier_than[s][t], weight[s] * front(s, (s, t)), 0.0)
        back[0].append(total)
        for c in range(3):
            back[c + 1].append(pulled[c] * prefix[t])
    spread_back = jnp.zeros((seg_dev, LANES), f32)
    for ch in range(4):
        spread_back = jnp.where(
            (lane >= ch * ROW) & (lane < (ch + 1) * ROW), jnp.concatenate(back[ch], 0), spread_back
        )
    spread_back = jnp.where(unit_mask, spread_back, 0.0)
    homeward = unwide(dot(owner_turned, wide(spread_back)))
    send_c[...] = jnp.zeros_like(send_c)
    for ch in range(4):
        moved = pltpu.roll(homeward, lax.rem(shift_home - ch * ROW + LANES, LANES), 1)
        send_c[:, ch, :] = jnp.where((lane_n >= shift_home) & (lane_n < shift_home + ROW), moved, 0.0)

    exchange_c = (n, me, "region", lambda p: send_c.at[p], recv_c, sem_c.at[0], sem_c.at[1])
    exchange_start(*exchange_c)
    recv_c[me] = send_c[me]
    exchange_wait(*exchange_c)

    groups = []
    for q in range(send_b.shape[0]):
        total = recv_c[q * GROUP]
        for k in range(1, min(GROUP, n)):
            total = total + recv_c[q * GROUP + k]
        groups.append(total)
    cotangent = tall(jnp.concatenate(groups, 1))
    for l in range(owned):
        cot[l] = untall(dot_nt(cotangent, place[l]))

    def exchange_r(l):
        return (m, mez, "replica", lambda p: part.at[l, p], part_recv.at[l], sem_rs.at[l, 0], sem_rs.at[l, 1])

    def exchange_g(l):
        return (m, mez, "replica", lambda p: grads_ref.at[l, mez], grads_ref.at[l], sem_ag.at[l, 0], sem_ag.at[l, 1])

    for l in range(owned):
        pull = cot[l]
        later = pull[0:1] * alpha[l, seg_len - 1][0:1]
        for i in range(seg_len - 1, -1, -1):
            emitted = shade[l, i]
            after = alpha[l, i]
            ahead = alpha[l, i - 1] if i > 0 else jnp.ones_like(after)
            share = ahead - after
            lit = pull * emitted
            lit = jnp.sum(jnp.where((sub >= 1) & (sub <= 3), lit, 0.0), axis=0, keepdims=True)
            later = later + lit * share[0:1]
            density = (lit * ahead[0:1] - later) * gaps[l][i : i + 1] * emitted[0:1]
            tint = pull * share * emitted * (1.0 - emitted)
            values = jnp.where(sub == 0, density, jnp.where(sub <= 3, tint, 0.0))
            raw_grad[i // 2, :, (i % 2) * slots : (i % 2 + 1) * slots] = tall(values)

        acc_in[...] = jnp.zeros_like(acc_in)
        acc_mid[...] = jnp.zeros_like(acc_mid)
        acc_out[...] = jnp.zeros_like(acc_out)
        head = jnp.concatenate([wb_out[l].astype(f32)] * 4, 0).astype(bf16)

        def backward(c, carry):
            one, two = hid_one[l, c], hid_two[l, c]
            acc_out[...] += dot(raw_grad[c], two)
            grad_two = jnp.where(two > 0, dot_tn(raw_grad[c], head), 0.0).astype(bf16)
            acc_mid[...] += dot_tn(one, grad_two)
            grad_one = jnp.where(one > 0, dot_nt(grad_two, wb_mid[l]), 0.0).astype(bf16)
            acc_in[...] += dot_tn(feat[l, c], grad_one)
            return carry

        lax.fori_loop(0, chunks, backward, 0)
        part[l] = jnp.concatenate([acc_in[...], acc_mid[...]], 0).astype(bf16).reshape(part.shape[1:])
        exchange_start(*exchange_r(l))
        summed = untall(acc_out[...])[:4]
        half = summed.shape[1] // 2
        out_send[l] = jnp.concatenate([summed[:, :half], summed[:, half:]], 0)

    exchange_o = (m, mez, "replica", lambda p: out_send, out_recv, sem_go.at[0], sem_go.at[1])
    exchange_start(*exchange_o)
    out_recv[mez] = out_send[...]

    for l in range(owned):
        part_recv[l, mez] = part[l, mez]
        exchange_wait(*exchange_r(l))
        total = part_recv[l, 0].astype(f32)
        for k in range(1, m):
            total = total + part_recv[l, k].astype(f32)
        grads_ref[l, mez] = total.astype(bf16)
        exchange_start(*exchange_g(l))
    exchange_wait(*exchange_o)
    total = out_recv[0]
    for k in range(1, m):
        total = total + out_recv[k]
    for l in range(owned):
        grad_out_ref[l] = jnp.concatenate([total[l, :4], total[l, 4:]], 1)
    for l in range(owned):
        exchange_wait(*exchange_g(l))


def on_device(positions, spacing, targets, seg_region, seg_rank, frequencies, w_in, w_mid, w_out):
    n, m = lax.axis_size("region"), lax.axis_size("replica")
    rays, segs = seg_rank.shape
    seg_len = positions.shape[2] // segs
    owned, enc, hid = w_in.shape
    cap = 3 * rays * segs // (owned * n)
    slots, chunk = n * cap, 2 * n * cap
    chunks = seg_len // 2
    rows = owned * cap
    groups = max(1, n // GROUP)
    deep = (enc + hid) // m
    half = w_out.shape[2] // 2
    vmem = pltpu.VMEM
    colour, grads, grad_out = pl.pallas_call(
        functools.partial(step_kernel, n, m, cap, segs, seg_len),
        out_shape=(
            jax.ShapeDtypeStruct((3, rays), f32),
            jax.ShapeDtypeStruct((owned, m, deep, hid), bf16),
            jax.ShapeDtypeStruct(w_out.shape, f32),
        ),
        in_specs=[pl.BlockSpec(memory_space=vmem)] * 9,
        out_specs=[pl.BlockSpec(memory_space=vmem)] * 3,
        scratch_shapes=[
            vmem((n, rows, LANES), f32),
            vmem((n, rows, LANES), f32),
            vmem((groups, 8, LANES), f32),
            vmem((n, 8, LANES), f32),
            vmem((n, 8, LANES), f32),
            vmem((n, 8, LANES), f32),
            vmem((owned, chunks, chunk, enc), bf16),
            vmem((owned, chunks, chunk, hid), bf16),
            vmem((owned, chunks, chunk, hid), bf16),
            vmem((chunks, 8, chunk), f32),
            vmem((owned, seg_len, 8, slots), f32),
            vmem((owned, seg_len, 8, slots), f32),
            vmem((owned, seg_len, slots), f32),
            vmem((owned, 8, slots), f32),
            vmem((chunks, 32, chunk), bf16),
            vmem((owned, slots, n * ROW), bf16),
            vmem((chunks, 2 * LANES, enc), bf16),
            vmem((chunks, LANES, enc), bf16),
            vmem((owned, slots, 2 * LANES), bf16),
            vmem((owned, enc, hid), bf16),
            vmem((owned, hid, hid), bf16),
            vmem((owned, 8, hid), bf16),
            vmem((enc, hid), f32),
            vmem((hid, hid), f32),
            vmem((32, hid), f32),
            vmem((owned, m, deep, hid), bf16),
            vmem((owned, m, deep, hid), bf16),
            vmem((owned, 8, half), f32),
            vmem((m, owned, 8, half), f32),
            pltpu.SemaphoreType.DMA((2, n)),
            pltpu.SemaphoreType.DMA((2, n)),
            pltpu.SemaphoreType.DMA((2, n)),
            pltpu.SemaphoreType.DMA((owned, 2, m)),
            pltpu.SemaphoreType.DMA((owned, 2, m)),
            pltpu.SemaphoreType.DMA((2, m)),
        ],
        compiler_params=pltpu.CompilerParams(
            collective_id=0, has_side_effects=True, vmem_limit_bytes=56 * 2**20
        ),
        name="radiance_step",
    )(positions, spacing, targets, seg_region.reshape(rays, segs), seg_rank, frequencies, w_in, w_mid, w_out)
    grads = grads.reshape(owned, enc + hid, hid)
    return (colour, grads[:, :enc].astype(f32), grads[:, enc:].astype(f32), grad_out)


def solution(mesh):
    in_specs = (
        P(None, ("region", "replica"), None),
        P(("region", "replica"), None),
        P(None, ("region", "replica")),
        P(("region", "replica"), None, None),
        P(("region", "replica"), None),
        P(),
        P("region", None, None),
        P("region", None, None),
        P("region", None, None),
    )
    out_specs = (
        P(None, ("region", "replica")),
        P("region", None, None),
        P("region", None, None),
        P("region", None, None),
    )
    return jax.shard_map(
        on_device, mesh=mesh, in_specs=in_specs, out_specs=out_specs, check_vma=False
    )
```

```python
import functools

import jax
import jax.numpy as jnp
from jax import lax
from jax.experimental import pallas as pl
from jax.experimental.pallas import tpu as pltpu
from jax.sharding import PartitionSpec as P

MESH = pl.DeviceIdType.MESH
f32, bf16 = jnp.float32, jnp.bfloat16
LANES = 128
ROW = 16
loss_scale = 16.0

SIN_HALF = (4.442882919048677, -7.308245676836255, 3.606354025126868, -0.8461104138552027, 0.10982204430121903)
COS_HALF = (1.4142134959439656, -6.978850908781684, 5.739459581977078, -1.8835528214703008, 0.31067786282805515)


def iota(shape, dim):
    return lax.broadcasted_iota(jnp.int32, shape, dim)


def dot(a, b):
    return jnp.dot(a, b, preferred_element_type=f32)


def dot_nt(a, b):
    return lax.dot_general(a, b, (((1,), (1,)), ((), ())), preferred_element_type=f32)


def dot_tn(a, b):
    return lax.dot_general(a, b, (((0,), (0,)), ((), ())), preferred_element_type=f32)


def split(x):
    high = x.astype(bf16).astype(f32)
    rest = x - high
    middle = rest.astype(bf16).astype(f32)
    return high, middle, rest - middle


def wide(x):
    return jnp.concatenate(split(x), 1).astype(bf16)


def tall(x):
    return jnp.concatenate((*split(x), jnp.zeros_like(x)), 0).astype(bf16)


def unwide(x):
    w = x.shape[1] // 3
    return x[:, :w] + x[:, w : 2 * w] + x[:, 2 * w :]


def untall(x):
    w = x.shape[0] // 4
    return x[:w] + x[w : 2 * w] + x[2 * w : 3 * w]


def polynomial(coefficients, z):
    value = jnp.full_like(z, coefficients[-1])
    for coefficient in coefficients[-2::-1]:
        value = value * z + coefficient
    return value


def sin_cos_turns(turns):
    rest = turns - jnp.round(turns)
    square = rest * rest
    s = polynomial(SIN_HALF, square) * rest
    c = polynomial(COS_HALF, square)
    return s * c, 1.0 - s * s


def column_from_row(eye, row):
    return jnp.sum(jnp.where(eye, jnp.broadcast_to(row, eye.shape), 0.0), axis=1, keepdims=True)


def on_lanes(x, width=LANES):
    return jnp.concatenate([x, jnp.zeros((x.shape[0], width - x.shape[1]), x.dtype)], 1)


def exchange_start(count, me, axis, source_of, target, send, recv):
    def start(k, carry):
        peer = lax.rem(me + k, count)
        pltpu.make_async_remote_copy(
            src_ref=source_of(peer),
            dst_ref=target.at[me],
            send_sem=send.at[k],
            recv_sem=recv.at[k],
            device_id={axis: peer},
            device_id_type=MESH,
        ).start()
        return carry

    lax.fori_loop(1, count, start, 0)


def exchange_wait(count, me, axis, source_of, target, send, recv):
    def wait(k, carry):
        peer = lax.rem(me + k, count)
        origin = lax.rem(me + count - k, count)
        pltpu.make_async_remote_copy(
            src_ref=source_of(peer),
            dst_ref=target.at[origin],
            send_sem=send.at[k],
            recv_sem=recv.at[k],
            device_id={axis: peer},
            device_id_type=MESH,
        ).wait()
        return carry

    lax.fori_loop(1, count, wait, 0)


def step_kernel(
    n, m, cap, segs, seg_len,
    pos_ref, gap_ref, tgt_ref, reg_ref, rank_ref, freq_ref, w_out_ref, w_in_hbm, w_mid_hbm,
    colour_ref, grads_ref, grad_out_ref,
    send_a, recv_a, send_b, recv_b, send_c, recv_c,
    feat, hid_one, hid_two, raw, shade, alpha, gaps, raw_grad, grad_two,
    place, phase_hi, phase_lo, slots_x, w_in, w_mid, wb_in, wb_mid, wb_out,
    acc, acc_out, part, part_recv, out_send, out_recv,
    sem_w, sem_a, sem_b, sem_c, sem_rs, sem_ag, sem_go,
):
    me = lax.axis_index("region")
    mez = lax.axis_index("replica")
    owned = w_in.shape[0]
    rays = pos_ref.shape[1]
    seg_dev = rays * segs
    slots = n * cap
    chunks = seg_len // 2
    per_tile = LANES // ROW
    half_lanes = LANES // 2

    barrier = pltpu.get_barrier_semaphore()

    def greet_region(k, carry):
        pl.semaphore_signal(
            barrier, inc=1, device_id={"region": lax.rem(me + k, n)}, device_id_type=MESH
        )
        return carry

    def greet_replica(k, carry):
        pl.semaphore_signal(
            barrier, inc=1, device_id={"replica": lax.rem(mez + k, m)}, device_id_type=MESH
        )
        return carry

    lax.fori_loop(1, n, greet_region, 0)
    lax.fori_loop(1, m, greet_replica, 0)
    load_in = pltpu.make_async_copy(w_in_hbm, w_in, sem_w.at[0])
    load_mid = pltpu.make_async_copy(w_mid_hbm, w_mid, sem_w.at[1])
    load_in.start()
    load_mid.start()

    eye = iota((rays, rays), 0) == iota((rays, rays), 1)
    region_col = jnp.concatenate([column_from_row(eye, reg_ref[s].astype(f32)) for s in range(segs)], 0)
    lane = iota((seg_dev, LANES), 1)
    onehot = jnp.where(region_col == lane.astype(f32), 1.0, 0.0)
    before = jnp.where(iota((seg_dev, seg_dev), 0) > iota((seg_dev, seg_dev), 1), 1.0, 0.0)
    earlier = dot(before.astype(bf16), onehot.astype(bf16))
    order_col = jnp.sum(earlier * onehot, axis=1, keepdims=True)
    owner_col = jnp.floor((region_col + 0.5) * (1.0 / owned))
    local_col = region_col - owned * owner_col
    keys = jnp.where(lane == 0, owner_col * ROW + order_col, jnp.where(lane == 1, owner_col, 0.0)).T
    slot_row, owner_row = keys[0:1, :], keys[1:2, :]

    pieces = []
    lane_s = iota((rays, LANES), 1) & (half_lanes - 1)
    for s in range(segs):
        packed = jnp.zeros((rays, LANES), f32)
        for d in range(4):
            source = on_lanes(pos_ref[d] if d < 3 else gap_ref[...].astype(f32))
            shift = seg_len * (d - s)
            moved = pltpu.roll(source, shift % LANES, 1)
            packed = jnp.where((lane_s >= seg_len * d) & (lane_s < seg_len * (d + 1)), moved, packed)
        pieces.append(packed[:, :])
    packed = jnp.concatenate(pieces, 0)
    packed = jnp.where(lane < half_lanes, packed, pltpu.roll(packed, half_lanes, 1))
    own_half = (lane >= half_lanes).astype(f32) == local_col
    packed = wide(jnp.where(own_half, packed, 0.0))
    scatter = jnp.where(iota((n * ROW, seg_dev), 0).astype(f32) == slot_row, 1.0, 0.0).astype(bf16)
    send_a[...] = unwide(dot(scatter, packed)).reshape(send_a.shape)

    pl.semaphore_wait(barrier, n - 1 + m - 1)
    exchange_a = (n, me, "region", lambda p: send_a.at[p], recv_a, sem_a.at[0], sem_a.at[1])
    exchange_start(*exchange_a)
    recv_a[me] = send_a[me]

    slot_id = iota((slots, 1), 0).astype(f32)
    peer_id = jnp.floor((slot_id + 0.5) * (1.0 / cap))
    spot = slot_id + (ROW - cap) * peer_id
    place[...] = jnp.where(iota((slots, n * ROW), 1).astype(f32) == spot, 1.0, 0.0).astype(bf16)
    freq_high, freq_middle, freq_low = split(freq_ref[...])
    width = freq_ref.shape[1]

    def spread(values):
        return jnp.concatenate([jnp.broadcast_to(values[d : d + 1], (seg_len, width)) for d in range(3)], 0)

    rest16 = jnp.zeros((seg_len, width), f32)
    rest32 = jnp.zeros((2 * seg_len, width), f32)
    table_hi = jnp.concatenate(
        [spread(freq_high), spread(freq_high), rest32, spread(freq_high), rest16, spread(freq_middle), rest16], 0
    )
    table_lo = jnp.concatenate([spread(freq_low), spread(freq_middle), rest32], 0)
    for i in range(seg_len):
        cols = slice((i % 2) * width, (i % 2 + 1) * width)
        mine = (iota(table_hi.shape, 0) & (seg_len - 1)) == i
        phase_hi[i // 2, :, cols] = jnp.where(mine, table_hi, 0.0).astype(bf16)
        mine = (iota(table_lo.shape, 0) & (seg_len - 1)) == i
        phase_lo[i // 2, :, cols] = jnp.where(mine, table_lo, 0.0).astype(bf16)
    load_in.wait()
    load_mid.wait()
    for l in range(owned):
        wb_in[l] = w_in[l].astype(bf16)
        wb_mid[l] = w_mid[l].astype(bf16)
        wb_out[l] = jnp.concatenate([w_out_ref[l], jnp.zeros((4, w_out_ref.shape[2]), f32)], 0).astype(bf16)

    exchange_wait(*exchange_a)

    high, middle, low = split(recv_a[...].reshape(n * ROW, LANES))
    lane_r = iota(high.shape, 1)
    coords = 3 * seg_len
    high_turned = pltpu.roll(high, half_lanes, 1)
    pick_gap = jnp.where(
        iota((seg_len, 2 * LANES), 1) == iota((seg_len, 2 * LANES), 0) + LANES + coords, 1.0, 0.0
    ).astype(bf16)
    for l in range(owned):
        own, other = (high, high_turned) if l == 0 else (high_turned, high)
        tail = low if l == 0 else pltpu.roll(low, half_lanes, 1)
        first = jnp.where(lane_r < coords, own, pltpu.roll(middle, coords + l * half_lanes, 1))
        second = jnp.where(lane_r < coords, tail, jnp.where(lane_r < half_lanes, own, other))
        slots_x[l] = dot(place[...], jnp.concatenate([first, second], 1).astype(bf16)).astype(bf16)
        gaps[l] = dot_nt(pick_gap, slots_x[l])

    def phases(l, c):
        return dot(slots_x[l], phase_hi[c]) + dot(slots_x[l][:, :LANES], phase_lo[c])

    def encode(l, c, turns):
        sines, cosines = sin_cos_turns(turns)
        for j in range(2):
            cols = slice(j * width, (j + 1) * width)
            feat[l, c, j * slots : (j + 1) * slots, :] = jnp.concatenate(
                [sines[:, cols], cosines[:, cols]], 1
            ).astype(bf16)

    def render(l):
        depth = jnp.zeros((8, slots), f32)
        clear = jnp.ones((8, slots), f32)
        colour = jnp.zeros((8, slots), f32)
        for i in range(seg_len):
            value = raw[l, i // 2][:, (i % 2) * slots : (i % 2 + 1) * slots]
            density = jnp.broadcast_to(value[0:1], value.shape)
            density = jnp.maximum(density, 0.0) + jnp.log1p(jnp.exp(-jnp.abs(density)))
            emitted = 1.0 / (1.0 + jnp.exp(-value))
            depth = depth + density * gaps[l][i : i + 1]
            after = jnp.exp(-depth)
            colour = colour + (clear - after) * emitted
            clear = after
            shade[l, i] = emitted
            alpha[l, i] = after
        return jnp.where(sub == 0, clear, colour)[:4]

    sub = iota((8, slots), 0)
    steps = [(l, c) for l in range(owned) for c in range(chunks)]
    encode(*steps[0], phases(*steps[0]))
    rendered = []
    for at, (l, c) in enumerate(steps):
        ahead = steps[at + 1] if at + 1 < len(steps) else None
        if ahead:
            turns = phases(*ahead)
        one = jnp.maximum(dot(feat[l, c], wb_in[l]), 0.0).astype(bf16)
        hid_one[l, c] = one
        if ahead:
            encode(*ahead, turns)
        two = jnp.maximum(dot(one, wb_mid[l]), 0.0).astype(bf16)
        hid_two[l, c] = two
        raw[l, c] = dot_nt(wb_out[l], two)
        if c == chunks - 1:
            rendered.append(render(l))
    returned = untall(dot(tall(jnp.concatenate(rendered, 0)), place[...]))
    for q in range(send_b.shape[0]):
        send_b[q] = returned[:, q * LANES : (q + 1) * LANES]

    exchange_b = (n, me, "region", lambda p: send_b.at[p // per_tile], recv_b, sem_b.at[0], sem_b.at[1])
    exchange_start(*exchange_b)
    recv_b[me] = send_b[me // per_tile]

    unit_mask = ((lane & (ROW - 1)).astype(f32) == order_col) & own_half
    channel = (lane // ROW) & 3
    owner_mask = jnp.where(iota((seg_dev, n), 1).astype(f32) == owner_col, 1.0, 0.0).astype(bf16)
    owner_turned = jnp.where(iota((n, seg_dev), 0).astype(f32) == owner_row, 1.0, 0.0).astype(bf16)
    rank = [column_from_row(eye, rank_ref[s : s + 1, :].astype(f32)) for s in range(segs)]
    earlier_than = [[rank[t] < rank[s] for t in range(segs)] for s in range(segs)]
    target = [column_from_row(eye, tgt_ref[c : c + 1, :]) for c in range(3)]
    shift_home = lax.rem(me, per_tile) * ROW

    exchange_wait(*exchange_b)

    lane_n = iota((n, LANES), 1)
    mine = jnp.zeros((n, LANES), f32)
    for ch in range(8):
        moved = pltpu.roll(recv_b[:, ch, :], lax.rem(ch * ROW - shift_home + LANES, LANES), 1)
        mine = jnp.where((lane_n >= ch * ROW) & (lane_n < (ch + 1) * ROW), moved, mine)
    found = jnp.where(unit_mask, unwide(dot(owner_mask, wide(mine))), 0.0)
    columns = [jnp.sum(jnp.where(channel == ch, found, 0.0), axis=1, keepdims=True) for ch in range(4)]
    by_seg = [[col[s * rays : (s + 1) * rays] for s in range(segs)] for col in columns]
    trans, colours = by_seg[0], by_seg[1:]

    def front(s, skip):
        product = jnp.ones((rays, 1), f32)
        for t in range(segs):
            if t not in skip:
                product = product * jnp.where(earlier_than[s][t], trans[t], 1.0)
        return product

    prefix = [front(s, (s,)) for s in range(segs)]
    pulled = []
    for c in range(3):
        total = colours[c][0] * prefix[0]
        for s in range(1, segs):
            total = total + colours[c][s] * prefix[s]
        colour_ref[c : c + 1, :] = jnp.sum(
            jnp.where(eye, jnp.broadcast_to(total, eye.shape), 0.0), axis=0, keepdims=True
        )
        pulled.append((2.0 * loss_scale) * (total - target[c]))
    weight = [
        pulled[0] * colours[0][s] + pulled[1] * colours[1][s] + pulled[2] * colours[2][s] for s in range(segs)
    ]
    back = [[], [], [], []]
    for t in range(segs):
        total = jnp.zeros((rays, 1), f32)
        for s in range(segs):
            if s != t:
                total = total + jnp.where(earlier_than[s][t], weight[s] * front(s, (s, t)), 0.0)
        back[0].append(total)
        for c in range(3):
            back[c + 1].append(pulled[c] * prefix[t])
    spread_back = jnp.zeros((seg_dev, LANES), f32)
    for ch in range(4):
        spread_back = jnp.where(channel == ch, jnp.concatenate(back[ch], 0), spread_back)
    spread_back = jnp.where(unit_mask, spread_back, 0.0)
    homeward = unwide(dot(owner_turned, wide(spread_back)))
    for ch in range(8):
        moved = pltpu.roll(homeward, lax.rem(shift_home - ch * ROW + LANES, LANES), 1)
        send_c[:, ch, :] = jnp.where((lane_n >= shift_home) & (lane_n < shift_home + ROW), moved, 0.0)

    exchange_c = (n, me, "region", lambda p: send_c.at[p], recv_c, sem_c.at[0], sem_c.at[1])
    exchange_start(*exchange_c)
    recv_c[me] = send_c[me]
    exchange_wait(*exchange_c)

    groups = []
    for q in range(send_b.shape[0]):
        total = recv_c[q * per_tile]
        for k in range(1, per_tile):
            total = total + recv_c[q * per_tile + k]
        groups.append(total)
    cotangent = untall(dot_nt(tall(jnp.concatenate(groups, 1)), place[...]))

    def render_back(l):
        pull = cotangent if l == 0 else pltpu.roll(cotangent, 4, 0)
        later = pull[0:1] * alpha[l, seg_len - 1][0:1]
        for i in range(seg_len - 1, -1, -1):
            emitted = shade[l, i]
            after = alpha[l, i]
            ahead = alpha[l, i - 1] if i > 0 else jnp.ones_like(after)
            share = ahead - after
            lit = pull * emitted
            lit = jnp.sum(jnp.where((sub >= 1) & (sub <= 3), lit, 0.0), axis=0, keepdims=True)
            later = later + lit * share[0:1]
            density = (lit * ahead[0:1] - later) * gaps[l][i : i + 1] * emitted[0:1]
            tint = pull * share * emitted * (1.0 - emitted)
            values = jnp.where(sub == 0, density, jnp.where(sub <= 3, tint, 0.0))
            raw_grad[l, i // 2, :, (i % 2) * slots : (i % 2 + 1) * slots] = tall(values)

    def exchange_r(p):
        return (m, mez, "replica", lambda z: part.at[p, z], part_recv.at[p], sem_rs.at[p, 0], sem_rs.at[p, 1])

    def exchange_g(p):
        return (m, mez, "replica", lambda z: grads_ref.at[p, mez], grads_ref.at[p], sem_ag.at[p, 0], sem_ag.at[p, 1])

    def send_part(p):
        part[p] = acc[...].astype(bf16).reshape(part.shape[1:])
        exchange_start(*exchange_r(p))

    def sum_part(p):
        part_recv[p, mez] = part[p, mez]
        exchange_wait(*exchange_r(p))
        total = part_recv[p, 0].astype(f32)
        for k in range(1, m):
            total = total + part_recv[p, k].astype(f32)
        grads_ref[p, mez] = total.astype(bf16)
        exchange_start(*exchange_g(p))

    for l in range(owned):
        render_back(l)
    for l in range(owned):
        head = jnp.concatenate([wb_out[l].astype(f32)] * 4, 0).astype(bf16)

        def second_grad(c):
            grad_two[l, c] = jnp.where(hid_two[l, c] > 0, dot_tn(raw_grad[l, c], head), 0.0).astype(bf16)

        def first_grad(c):
            return jnp.where(hid_one[l, c] > 0, dot_nt(grad_two[l, c], wb_mid[l]), 0.0).astype(bf16)

        second_grad(0)
        for c in range(chunks):
            if c + 1 < chunks:
                second_grad(c + 1)
            term = dot_tn(hid_one[l, c], grad_two[l, c])
            acc[...] = term if c == 0 else acc[...] + term
            term = dot(raw_grad[l, c], hid_two[l, c])
            acc_out[...] = term if c == 0 else acc_out[...] + term
        send_part(2 * l)
        summed = untall(acc_out[...])[:4]
        half = summed.shape[1] // 2
        out_send[l] = jnp.concatenate([summed[:, :half], summed[:, half:]], 0)
        if l > 0:
            sum_part(2 * l - 2)
        now = first_grad(0)
        for c in range(chunks):
            later = first_grad(c + 1) if c + 1 < chunks else None
            term = dot_tn(feat[l, c], now)
            acc[...] = term if c == 0 else acc[...] + term
            now = later
        send_part(2 * l + 1)

    exchange_o = (m, mez, "replica", lambda z: out_send, out_recv, sem_go.at[0], sem_go.at[1])
    exchange_start(*exchange_o)
    out_recv[mez] = out_send[...]
    for p in range(2 * owned - 3, 2 * owned):
        sum_part(p)
    exchange_wait(*exchange_o)
    total = out_recv[0]
    for k in range(1, m):
        total = total + out_recv[k]
    for l in range(owned):
        grad_out_ref[l] = jnp.concatenate([total[l, :4], total[l, 4:]], 1)
    for p in range(2 * owned):
        exchange_wait(*exchange_g(p))


def finish_kernel(colour, grads, grad_out, colour_ref, grad_in_ref, grad_mid_ref, grad_out_ref):
    colour_ref[...] = colour[...]
    grad_out_ref[...] = grad_out[...]
    for l in range(grad_in_ref.shape[0]):
        grad_mid_ref[l] = grads[2 * l].astype(f32)
        grad_in_ref[l] = grads[2 * l + 1].astype(f32)


def on_device(positions, spacing, targets, seg_region, seg_rank, frequencies, w_in, w_mid, w_out):
    n, m = lax.axis_size("region"), lax.axis_size("replica")
    rays, segs = seg_rank.shape
    seg_len = positions.shape[2] // segs
    owned, enc, hid = w_in.shape
    cap = 3 * rays * segs // (owned * n)
    slots, chunk = n * cap, 2 * n * cap
    chunks = seg_len // 2
    groups = n * ROW // LANES
    deep = hid // m
    half = w_out.shape[2] // 2
    vmem = pltpu.VMEM
    semaphores = pltpu.SemaphoreType.DMA
    colour, grads, grad_out = pl.pallas_call(
        functools.partial(step_kernel, n, m, cap, segs, seg_len),
        out_shape=(
            jax.ShapeDtypeStruct((3, rays), f32),
            jax.ShapeDtypeStruct((2 * owned, m, deep, hid), bf16),
            jax.ShapeDtypeStruct(w_out.shape, f32),
        ),
        in_specs=[pl.BlockSpec(memory_space=vmem)] * 7 + [pl.BlockSpec(memory_space=pl.ANY)] * 2,
        out_specs=[pl.BlockSpec(memory_space=vmem)] * 3,
        scratch_shapes=[
            vmem((n, ROW, LANES), f32),
            vmem((n, ROW, LANES), f32),
            vmem((groups, 8, LANES), f32),
            vmem((n, 8, LANES), f32),
            vmem((n, 8, LANES), f32),
            vmem((n, 8, LANES), f32),
            vmem((owned, chunks, chunk, enc), bf16),
            vmem((owned, chunks, chunk, hid), bf16),
            vmem((owned, chunks, chunk, hid), bf16),
            vmem((owned, chunks, 8, chunk), f32),
            vmem((owned, seg_len, 8, slots), f32),
            vmem((owned, seg_len, 8, slots), f32),
            vmem((owned, seg_len, slots), f32),
            vmem((owned, chunks, 32, chunk), bf16),
            vmem((owned, chunks, chunk, hid), bf16),
            vmem((slots, n * ROW), bf16),
            vmem((chunks, 2 * LANES, enc), bf16),
            vmem((chunks, LANES, enc), bf16),
            vmem((owned, slots, 2 * LANES), bf16),
            vmem((owned, enc, hid), f32),
            vmem((owned, hid, hid), f32),
            vmem((owned, enc, hid), bf16),
            vmem((owned, hid, hid), bf16),
            vmem((owned, 8, hid), bf16),
            vmem((hid, hid), f32),
            vmem((32, hid), f32),
            vmem((2 * owned, m, deep, hid), bf16),
            vmem((2 * owned, m, deep, hid), bf16),
            vmem((owned, 8, half), f32),
            vmem((m, owned, 8, half), f32),
            semaphores((2,)),
            semaphores((2, n)),
            semaphores((2, n)),
            semaphores((2, n)),
            semaphores((2 * owned, 2, m)),
            semaphores((2 * owned, 2, m)),
            semaphores((2, m)),
        ],
        compiler_params=pltpu.CompilerParams(
            collective_id=0, has_side_effects=True, vmem_limit_bytes=56 * 2**20
        ),
        name="radiance_step",
    )(
        positions, spacing, targets, seg_region.transpose(1, 2, 0), seg_rank.T, frequencies, w_out, w_in, w_mid
    )
    return pl.pallas_call(
        finish_kernel,
        out_shape=(
            jax.ShapeDtypeStruct(colour.shape, f32),
            jax.ShapeDtypeStruct(w_in.shape, f32),
            jax.ShapeDtypeStruct(w_mid.shape, f32),
            jax.ShapeDtypeStruct(w_out.shape, f32),
        ),
        in_specs=[pl.BlockSpec(memory_space=vmem)] * 3,
        out_specs=[pl.BlockSpec(memory_space=vmem)] * 4,
        name="widen",
    )(colour, grads.reshape(2 * owned, hid, hid), grad_out)


def solution(mesh):
    in_specs = (
        P(None, ("region", "replica"), None),
        P(("region", "replica"), None),
        P(None, ("region", "replica")),
        P(("region", "replica"), None, None),
        P(("region", "replica"), None),
        P(),
        P("region", None, None),
        P("region", None, None),
        P("region", None, None),
    )
    out_specs = (
        P(None, ("region", "replica")),
        P("region", None, None),
        P("region", None, None),
        P("region", None, None),
    )
    return jax.shard_map(
        on_device, mesh=mesh, in_specs=in_specs, out_specs=out_specs, check_vma=False
    )
```

```python
import functools

import jax
import jax.numpy as jnp
from jax import lax
from jax.experimental import pallas as pl
from jax.experimental.pallas import tpu as pltpu
from jax.sharding import PartitionSpec as P

MESH = pl.DeviceIdType.MESH
f32, bf16 = jnp.float32, jnp.bfloat16
LANES = 128
ROW = 16
loss_scale = 16.0

SIN_HALF = (4.442882919048677, -7.308245676836255, 3.606354025126868, -0.8461104138552027, 0.10982204430121903)
COS_HALF = (1.4142134959439656, -6.978850908781684, 5.739459581977078, -1.8835528214703008, 0.31067786282805515)


def iota(shape, dim):
    return lax.broadcasted_iota(jnp.int32, shape, dim)


def dot(a, b):
    return jnp.dot(a, b, preferred_element_type=f32)


def dot_nt(a, b):
    return lax.dot_general(a, b, (((1,), (1,)), ((), ())), preferred_element_type=f32)


def dot_tn(a, b):
    return lax.dot_general(a, b, (((0,), (0,)), ((), ())), preferred_element_type=f32)


def split(x):
    high = x.astype(bf16).astype(f32)
    rest = x - high
    middle = rest.astype(bf16).astype(f32)
    return high, middle, rest - middle


def wide(x):
    return jnp.concatenate(split(x), 1).astype(bf16)


def tall(x):
    return jnp.concatenate((*split(x), jnp.zeros_like(x)), 0).astype(bf16)


def unwide(x):
    w = x.shape[1] // 3
    return x[:, :w] + x[:, w : 2 * w] + x[:, 2 * w :]


def untall(x):
    w = x.shape[0] // 4
    return x[:w] + x[w : 2 * w] + x[2 * w : 3 * w]


def polynomial(coefficients, z):
    value = jnp.full_like(z, coefficients[-1])
    for coefficient in coefficients[-2::-1]:
        value = value * z + coefficient
    return value


def sin_cos_turns(turns):
    rest = turns - jnp.round(turns)
    square = rest * rest
    s = polynomial(SIN_HALF, square) * rest
    c = polynomial(COS_HALF, square)
    return s * c, 1.0 - s * s


def column_from_row(eye, row):
    return jnp.sum(jnp.where(eye, jnp.broadcast_to(row, eye.shape), 0.0), axis=1, keepdims=True)


def on_lanes(x, width=LANES):
    return jnp.concatenate([x, jnp.zeros((x.shape[0], width - x.shape[1]), x.dtype)], 1)


def exchange_start(count, me, axis, source_of, target, send, recv):
    def start(k, carry):
        peer = lax.rem(me + k, count)
        pltpu.make_async_remote_copy(
            src_ref=source_of(peer),
            dst_ref=target.at[me],
            send_sem=send.at[k],
            recv_sem=recv.at[k],
            device_id={axis: peer},
            device_id_type=MESH,
        ).start()
        return carry

    lax.fori_loop(1, count, start, 0)


def exchange_wait(count, me, axis, source_of, target, send, recv):
    def wait(k, carry):
        peer = lax.rem(me + k, count)
        origin = lax.rem(me + count - k, count)
        pltpu.make_async_remote_copy(
            src_ref=source_of(peer),
            dst_ref=target.at[origin],
            send_sem=send.at[k],
            recv_sem=recv.at[k],
            device_id={axis: peer},
            device_id_type=MESH,
        ).wait()
        return carry

    lax.fori_loop(1, count, wait, 0)


def step_kernel(
    n, m, cap, segs, seg_len,
    pos_ref, gap_ref, tgt_ref, reg_ref, rank_ref, freq_ref, w_out_ref, w_in_hbm, w_mid_hbm,
    colour_ref, grads_ref, grad_out_ref,
    send_a, recv_a, send_b, recv_b, send_c, recv_c,
    feat, hid_one, hid_two, raw, shade, alpha, gaps, raw_grad, grad_two, feat_t, one_t,
    place, phase_hi, phase_lo, slots_x, w_in, w_mid, wb_in, wb_mid, wb_out, wb_out_t,
    acc, acc_out, part, part_recv, out_send, out_recv,
    sem_w, sem_a, sem_b, sem_c, sem_rs, sem_ag, sem_go,
):
    me = lax.axis_index("region")
    mez = lax.axis_index("replica")
    owned = w_in.shape[0]
    rays = pos_ref.shape[1]
    seg_dev = rays * segs
    slots = n * cap
    chunks = seg_len // 2
    per_tile = LANES // ROW
    half_lanes = LANES // 2

    barrier = pltpu.get_barrier_semaphore()

    def greet_region(k, carry):
        pl.semaphore_signal(
            barrier, inc=1, device_id={"region": lax.rem(me + k, n)}, device_id_type=MESH
        )
        return carry

    def greet_replica(k, carry):
        pl.semaphore_signal(
            barrier, inc=1, device_id={"replica": lax.rem(mez + k, m)}, device_id_type=MESH
        )
        return carry

    lax.fori_loop(1, n, greet_region, 0)
    lax.fori_loop(1, m, greet_replica, 0)
    load_in = pltpu.make_async_copy(w_in_hbm, w_in, sem_w.at[0])
    load_mid = pltpu.make_async_copy(w_mid_hbm, w_mid, sem_w.at[1])
    load_in.start()
    load_mid.start()

    eye = iota((rays, rays), 0) == iota((rays, rays), 1)
    region_col = jnp.concatenate([column_from_row(eye, reg_ref[s].astype(f32)) for s in range(segs)], 0)
    lane = iota((seg_dev, LANES), 1)
    onehot = jnp.where(region_col == lane.astype(f32), 1.0, 0.0)
    before = jnp.where(iota((seg_dev, seg_dev), 0) > iota((seg_dev, seg_dev), 1), 1.0, 0.0)
    earlier = dot(before.astype(bf16), onehot.astype(bf16))
    order_col = jnp.sum(earlier * onehot, axis=1, keepdims=True)
    owner_col = jnp.floor((region_col + 0.5) * (1.0 / owned))
    local_col = region_col - owned * owner_col
    keys = jnp.where(lane == 0, owner_col * ROW + order_col, jnp.where(lane == 1, owner_col, 0.0)).T
    slot_row, owner_row = keys[0:1, :], keys[1:2, :]

    pieces = []
    lane_s = iota((rays, LANES), 1) & (half_lanes - 1)
    for s in range(segs):
        packed = jnp.zeros((rays, LANES), f32)
        for d in range(4):
            source = on_lanes(pos_ref[d] if d < 3 else gap_ref[...].astype(f32))
            shift = seg_len * (d - s)
            moved = pltpu.roll(source, shift % LANES, 1)
            packed = jnp.where((lane_s >= seg_len * d) & (lane_s < seg_len * (d + 1)), moved, packed)
        pieces.append(packed[:, :])
    packed = jnp.concatenate(pieces, 0)
    packed = jnp.where(lane < half_lanes, packed, pltpu.roll(packed, half_lanes, 1))
    own_half = (lane >= half_lanes).astype(f32) == local_col
    packed = wide(jnp.where(own_half, packed, 0.0))
    scatter = jnp.where(iota((n * ROW, seg_dev), 0).astype(f32) == slot_row, 1.0, 0.0).astype(bf16)
    send_a[...] = unwide(dot(scatter, packed)).reshape(send_a.shape)

    pl.semaphore_wait(barrier, n - 1 + m - 1)
    exchange_a = (n, me, "region", lambda p: send_a.at[p], recv_a, sem_a.at[0], sem_a.at[1])
    exchange_start(*exchange_a)
    recv_a[me] = send_a[me]

    slot_id = iota((slots, 1), 0).astype(f32)
    peer_id = jnp.floor((slot_id + 0.5) * (1.0 / cap))
    spot = slot_id + (ROW - cap) * peer_id
    place[...] = jnp.where(iota((slots, n * ROW), 1).astype(f32) == spot, 1.0, 0.0).astype(bf16)
    freq_high, freq_middle, freq_low = split(freq_ref[...])
    width = freq_ref.shape[1]

    def spread(values):
        return jnp.concatenate([jnp.broadcast_to(values[d : d + 1], (seg_len, width)) for d in range(3)], 0)

    rest16 = jnp.zeros((seg_len, width), f32)
    rest32 = jnp.zeros((2 * seg_len, width), f32)
    table_hi = jnp.concatenate(
        [spread(freq_high), spread(freq_high), rest32, spread(freq_high), rest16, spread(freq_middle), rest16], 0
    )
    table_lo = jnp.concatenate([spread(freq_low), spread(freq_middle), rest32], 0)
    for i in range(seg_len):
        cols = slice((i % 2) * width, (i % 2 + 1) * width)
        mine = (iota(table_hi.shape, 0) & (seg_len - 1)) == i
        phase_hi[i // 2, :, cols] = jnp.where(mine, table_hi, 0.0).astype(bf16)
        mine = (iota(table_lo.shape, 0) & (seg_len - 1)) == i
        phase_lo[i // 2, :, cols] = jnp.where(mine, table_lo, 0.0).astype(bf16)
    load_in.wait()
    load_mid.wait()
    for l in range(owned):
        wb_in[l] = w_in[l].astype(bf16)
        wb_mid[l] = w_mid[l].astype(bf16)
        out_rows = jnp.concatenate([w_out_ref[l], jnp.zeros((LANES - 4, w_out_ref.shape[2]), f32)], 0)
        wb_out[l] = out_rows[:8].astype(bf16)
        wb_out_t[l] = out_rows.T.astype(bf16)

    exchange_wait(*exchange_a)

    high, middle, low = split(recv_a[...].reshape(n * ROW, LANES))
    lane_r = iota(high.shape, 1)
    coords = 3 * seg_len
    high_turned = pltpu.roll(high, half_lanes, 1)
    pick_gap = jnp.where(
        iota((seg_len, 2 * LANES), 1) == iota((seg_len, 2 * LANES), 0) + LANES + coords, 1.0, 0.0
    ).astype(bf16)
    for l in range(owned):
        own, other = (high, high_turned) if l == 0 else (high_turned, high)
        tail = low if l == 0 else pltpu.roll(low, half_lanes, 1)
        first = jnp.where(lane_r < coords, own, pltpu.roll(middle, coords + l * half_lanes, 1))
        second = jnp.where(lane_r < coords, tail, jnp.where(lane_r < half_lanes, own, other))
        slots_x[l] = dot(place[...], jnp.concatenate([first, second], 1).astype(bf16)).astype(bf16)
        gaps[l] = dot_nt(pick_gap, slots_x[l])

    def phases(l, c):
        return dot(slots_x[l], phase_hi[c]) + dot(slots_x[l][:, :LANES], phase_lo[c])

    def encode(l, c, turns):
        sines, cosines = sin_cos_turns(turns)
        for j in range(2):
            cols = slice(j * width, (j + 1) * width)
            feat[l, c, j * slots : (j + 1) * slots, :] = jnp.concatenate(
                [sines[:, cols], cosines[:, cols]], 1
            ).astype(bf16)

    def render(l):
        depth = jnp.zeros((8, slots), f32)
        clear = jnp.ones((8, slots), f32)
        colour = jnp.zeros((8, slots), f32)
        for i in range(seg_len):
            value = raw[l, i // 2][:, (i % 2) * slots : (i % 2 + 1) * slots]
            density = jnp.broadcast_to(value[0:1], value.shape)
            density = jnp.maximum(density, 0.0) + jnp.log1p(jnp.exp(-jnp.abs(density)))
            emitted = 1.0 / (1.0 + jnp.exp(-value))
            depth = depth + density * gaps[l][i : i + 1]
            after = jnp.exp(-depth)
            colour = colour + (clear - after) * emitted
            clear = after
            shade[l, i] = emitted
            alpha[l, i] = after
        return jnp.where(sub == 0, clear, colour)[:4]

    sub = iota((8, slots), 0)
    steps = [(l, c) for l in range(owned) for c in range(chunks)]
    encode(*steps[0], phases(*steps[0]))
    rendered = []
    for at, (l, c) in enumerate(steps):
        ahead = steps[at + 1] if at + 1 < len(steps) else None
        if ahead:
            turns = phases(*ahead)
        one = jnp.maximum(dot(feat[l, c], wb_in[l]), 0.0).astype(bf16)
        hid_one[l, c] = one
        if ahead:
            encode(*ahead, turns)
        two = jnp.maximum(dot(one, wb_mid[l]), 0.0).astype(bf16)
        hid_two[l, c] = two
        raw[l, c] = dot(two, wb_out_t[l]).T[:8]
        if c == chunks - 1:
            rendered.append(render(l))
    returned = untall(dot(tall(jnp.concatenate(rendered, 0)), place[...]))
    for q in range(send_b.shape[0]):
        send_b[q] = returned[:, q * LANES : (q + 1) * LANES]

    exchange_b = (n, me, "region", lambda p: send_b.at[p // per_tile], recv_b, sem_b.at[0], sem_b.at[1])
    exchange_start(*exchange_b)
    recv_b[me] = send_b[me // per_tile]

    unit_mask = ((lane & (ROW - 1)).astype(f32) == order_col) & own_half
    channel = (lane // ROW) & 3
    owner_mask = jnp.where(iota((seg_dev, n), 1).astype(f32) == owner_col, 1.0, 0.0).astype(bf16)
    owner_turned = jnp.where(iota((n, seg_dev), 0).astype(f32) == owner_row, 1.0, 0.0).astype(bf16)
    rank = [column_from_row(eye, rank_ref[s : s + 1, :].astype(f32)) for s in range(segs)]
    earlier_than = [[rank[t] < rank[s] for t in range(segs)] for s in range(segs)]
    target = [column_from_row(eye, tgt_ref[c : c + 1, :]) for c in range(3)]
    shift_home = lax.rem(me, per_tile) * ROW

    for l in range(owned):
        for c in range(chunks):
            one_t[l, c] = hid_one[l, c].T

    exchange_wait(*exchange_b)

    lane_n = iota((n, LANES), 1)
    mine = jnp.zeros((n, LANES), f32)
    for ch in range(8):
        moved = pltpu.roll(recv_b[:, ch, :], lax.rem(ch * ROW - shift_home + LANES, LANES), 1)
        mine = jnp.where((lane_n >= ch * ROW) & (lane_n < (ch + 1) * ROW), moved, mine)
    found = jnp.where(unit_mask, unwide(dot(owner_mask, wide(mine))), 0.0)
    columns = [jnp.sum(jnp.where(channel == ch, found, 0.0), axis=1, keepdims=True) for ch in range(4)]
    by_seg = [[col[s * rays : (s + 1) * rays] for s in range(segs)] for col in columns]
    trans, colours = by_seg[0], by_seg[1:]

    def front(s, skip):
        product = jnp.ones((rays, 1), f32)
        for t in range(segs):
            if t not in skip:
                product = product * jnp.where(earlier_than[s][t], trans[t], 1.0)
        return product

    prefix = [front(s, (s,)) for s in range(segs)]
    pulled = []
    for c in range(3):
        total = colours[c][0] * prefix[0]
        for s in range(1, segs):
            total = total + colours[c][s] * prefix[s]
        colour_ref[c : c + 1, :] = jnp.sum(
            jnp.where(eye, jnp.broadcast_to(total, eye.shape), 0.0), axis=0, keepdims=True
        )
        pulled.append((2.0 * loss_scale) * (total - target[c]))
    weight = [
        pulled[0] * colours[0][s] + pulled[1] * colours[1][s] + pulled[2] * colours[2][s] for s in range(segs)
    ]
    back = [[], [], [], []]
    for t in range(segs):
        total = jnp.zeros((rays, 1), f32)
        for s in range(segs):
            if s != t:
                total = total + jnp.where(earlier_than[s][t], weight[s] * front(s, (s, t)), 0.0)
        back[0].append(total)
        for c in range(3):
            back[c + 1].append(pulled[c] * prefix[t])
    spread_back = jnp.zeros((seg_dev, LANES), f32)
    for ch in range(4):
        spread_back = jnp.where(channel == ch, jnp.concatenate(back[ch], 0), spread_back)
    spread_back = jnp.where(unit_mask, spread_back, 0.0)
    homeward = unwide(dot(owner_turned, wide(spread_back)))
    for ch in range(8):
        moved = pltpu.roll(homeward, lax.rem(shift_home - ch * ROW + LANES, LANES), 1)
        send_c[:, ch, :] = jnp.where((lane_n >= shift_home) & (lane_n < shift_home + ROW), moved, 0.0)

    exchange_c = (n, me, "region", lambda p: send_c.at[p], recv_c, sem_c.at[0], sem_c.at[1])
    exchange_start(*exchange_c)
    recv_c[me] = send_c[me]
    for l in range(owned):
        for c in range(chunks):
            feat_t[l, c] = feat[l, c].T
    exchange_wait(*exchange_c)

    groups = []
    for q in range(send_b.shape[0]):
        total = recv_c[q * per_tile]
        for k in range(1, per_tile):
            total = total + recv_c[q * per_tile + k]
        groups.append(total)
    cotangent = untall(dot_nt(tall(jnp.concatenate(groups, 1)), place[...]))

    def render_back(l):
        pull = cotangent if l == 0 else pltpu.roll(cotangent, 4, 0)
        later = pull[0:1] * alpha[l, seg_len - 1][0:1]
        for i in range(seg_len - 1, -1, -1):
            emitted = shade[l, i]
            after = alpha[l, i]
            ahead = alpha[l, i - 1] if i > 0 else jnp.ones_like(after)
            share = ahead - after
            lit = pull * emitted
            lit = jnp.sum(jnp.where((sub >= 1) & (sub <= 3), lit, 0.0), axis=0, keepdims=True)
            later = later + lit * share[0:1]
            density = (lit * ahead[0:1] - later) * gaps[l][i : i + 1] * emitted[0:1]
            tint = pull * share * emitted * (1.0 - emitted)
            values = jnp.where(sub == 0, density, jnp.where(sub <= 3, tint, 0.0))
            raw_grad[l, i // 2, :, (i % 2) * slots : (i % 2 + 1) * slots] = tall(values)

    def exchange_r(p):
        return (m, mez, "replica", lambda z: part.at[p, z], part_recv.at[p], sem_rs.at[p, 0], sem_rs.at[p, 1])

    def exchange_g(p):
        return (m, mez, "replica", lambda z: grads_ref.at[p, mez], grads_ref.at[p], sem_ag.at[p, 0], sem_ag.at[p, 1])

    def send_part(p):
        part[p] = acc[...].astype(bf16).reshape(part.shape[1:])
        exchange_start(*exchange_r(p))

    def sum_part(p):
        part_recv[p, mez] = part[p, mez]
        exchange_wait(*exchange_r(p))
        total = part_recv[p, 0].astype(f32)
        for k in range(1, m):
            total = total + part_recv[p, k].astype(f32)
        grads_ref[p, mez] = total.astype(bf16)

    two_steps = m == 8
    last = 2 * owned - 1

    def hop(p, k, chunk, target):
        return pltpu.make_async_remote_copy(
            src_ref=grads_ref.at[p, chunk],
            dst_ref=grads_ref.at[p, chunk],
            send_sem=sem_ag.at[p, 0, k],
            recv_sem=sem_ag.at[p, 1, k],
            device_id={"replica": target},
            device_id_type=MESH,
        )

    def away(distance):
        return lax.rem(mez + distance + m, m)

    side = 2 - 4 * lax.rem(mez, 2)
    near = ((0, 1), (1, -1), (2, 2), (3, -2))
    far = ((4, away(-2), away(1)), (5, away(2), away(-1)), (6, away(-side), away(side)))

    def gather_near(p):
        if p == last or not two_steps:
            exchange_start(*exchange_g(p))
            return
        for k, distance in near:
            hop(p, k, mez, away(distance)).start()

    def gather_far(p):
        if p == last or not two_steps:
            return
        for k, distance in near[2:]:
            hop(p, k, away(-distance), away(distance)).wait_recv()
        for k, chunk, target in far:
            hop(p, k, chunk, target).start()

    def gather_wait(p):
        if p == last or not two_steps:
            exchange_wait(*exchange_g(p))
            return
        for k, distance in near[:2]:
            hop(p, k, away(-distance), away(distance)).wait_recv()
        for k, distance in ((4, -3), (5, 3), (6, 4)):
            hop(p, k, away(distance), away(1)).wait_recv()
        for k, distance in near:
            hop(p, k, mez, away(distance)).wait_send()
        for k, chunk, target in far:
            hop(p, k, chunk, target).wait_send()

    for l in range(owned):
        render_back(l)
    for l in range(owned):
        head = jnp.concatenate([wb_out[l].astype(f32)] * 4, 0).astype(bf16)

        def second_grad(c):
            grad_two[l, c] = jnp.where(hid_two[l, c] > 0, dot_tn(raw_grad[l, c], head), 0.0).astype(bf16)

        def first_grad(c):
            return jnp.where(hid_one[l, c] > 0, dot_nt(grad_two[l, c], wb_mid[l]), 0.0).astype(bf16)

        second_grad(0)
        for c in range(chunks):
            if c + 1 < chunks:
                second_grad(c + 1)
            term = dot(one_t[l, c], grad_two[l, c])
            acc[...] = term if c == 0 else acc[...] + term
            term = dot(raw_grad[l, c], hid_two[l, c])
            acc_out[...] = term if c == 0 else acc_out[...] + term
        send_part(2 * l)
        summed = untall(acc_out[...])[:4]
        half = summed.shape[1] // 2
        out_send[l] = jnp.concatenate([summed[:, :half], summed[:, half:]], 0)
        if l > 0:
            sum_part(2 * l - 2)
            gather_near(2 * l - 2)
        now = first_grad(0)
        for c in range(chunks):
            later = first_grad(c + 1) if c + 1 < chunks else None
            term = dot(feat_t[l, c], now)
            acc[...] = term if c == 0 else acc[...] + term
            now = later
        send_part(2 * l + 1)

    exchange_o = (m, mez, "replica", lambda z: out_send, out_recv, sem_go.at[0], sem_go.at[1])
    exchange_start(*exchange_o)
    out_recv[mez] = out_send[...]
    for p in range(last - 2, last):
        sum_part(p)
        gather_near(p)
        gather_far(p - 1)
    gather_far(last - 1)
    sum_part(last)
    gather_near(last)
    exchange_wait(*exchange_o)
    total = out_recv[0]
    for k in range(1, m):
        total = total + out_recv[k]
    for l in range(owned):
        grad_out_ref[l] = jnp.concatenate([total[l, :4], total[l, 4:]], 1)
    for p in range(2 * owned):
        gather_wait(p)


def finish_kernel(colour, grads, grad_out, colour_ref, grad_in_ref, grad_mid_ref, grad_out_ref):
    colour_ref[...] = colour[...]
    grad_out_ref[...] = grad_out[...]
    for l in range(grad_in_ref.shape[0]):
        grad_mid_ref[l] = grads[2 * l].astype(f32)
        grad_in_ref[l] = grads[2 * l + 1].astype(f32)


def on_device(positions, spacing, targets, seg_region, seg_rank, frequencies, w_in, w_mid, w_out):
    n, m = lax.axis_size("region"), lax.axis_size("replica")
    rays, segs = seg_rank.shape
    seg_len = positions.shape[2] // segs
    owned, enc, hid = w_in.shape
    cap = 3 * rays * segs // (owned * n)
    slots, chunk = n * cap, 2 * n * cap
    chunks = seg_len // 2
    groups = n * ROW // LANES
    deep = hid // m
    half = w_out.shape[2] // 2
    vmem = pltpu.VMEM
    semaphores = pltpu.SemaphoreType.DMA
    colour, grads, grad_out = pl.pallas_call(
        functools.partial(step_kernel, n, m, cap, segs, seg_len),
        out_shape=(
            jax.ShapeDtypeStruct((3, rays), f32),
            jax.ShapeDtypeStruct((2 * owned, m, deep, hid), bf16),
            jax.ShapeDtypeStruct(w_out.shape, f32),
        ),
        in_specs=[pl.BlockSpec(memory_space=vmem)] * 7 + [pl.BlockSpec(memory_space=pl.ANY)] * 2,
        out_specs=[pl.BlockSpec(memory_space=vmem)] * 3,
        scratch_shapes=[
            vmem((n, ROW, LANES), f32),
            vmem((n, ROW, LANES), f32),
            vmem((groups, 8, LANES), f32),
            vmem((n, 8, LANES), f32),
            vmem((n, 8, LANES), f32),
            vmem((n, 8, LANES), f32),
            vmem((owned, chunks, chunk, enc), bf16),
            vmem((owned, chunks, chunk, hid), bf16),
            vmem((owned, chunks, chunk, hid), bf16),
            vmem((owned, chunks, 8, chunk), f32),
            vmem((owned, seg_len, 8, slots), f32),
            vmem((owned, seg_len, 8, slots), f32),
            vmem((owned, seg_len, slots), f32),
            vmem((owned, chunks, 32, chunk), bf16),
            vmem((owned, chunks, chunk, hid), bf16),
            vmem((owned, chunks, enc, chunk), bf16),
            vmem((owned, chunks, hid, chunk), bf16),
            vmem((slots, n * ROW), bf16),
            vmem((chunks, 2 * LANES, enc), bf16),
            vmem((chunks, LANES, enc), bf16),
            vmem((owned, slots, 2 * LANES), bf16),
            vmem((owned, enc, hid), f32),
            vmem((owned, hid, hid), f32),
            vmem((owned, enc, hid), bf16),
            vmem((owned, hid, hid), bf16),
            vmem((owned, 8, hid), bf16),
            vmem((owned, hid, LANES), bf16),
            vmem((hid, hid), f32),
            vmem((32, hid), f32),
            vmem((2 * owned, m, deep, hid), bf16),
            vmem((2 * owned, m, deep, hid), bf16),
            vmem((owned, 8, half), f32),
            vmem((m, owned, 8, half), f32),
            semaphores((2,)),
            semaphores((2, n)),
            semaphores((2, n)),
            semaphores((2, n)),
            semaphores((2 * owned, 2, m)),
            semaphores((2 * owned, 2, m)),
            semaphores((2, m)),
        ],
        compiler_params=pltpu.CompilerParams(
            collective_id=0, has_side_effects=True, vmem_limit_bytes=56 * 2**20
        ),
        name="radiance_step",
    )(
        positions, spacing, targets, seg_region.transpose(1, 2, 0), seg_rank.T, frequencies, w_out, w_in, w_mid
    )
    return pl.pallas_call(
        finish_kernel,
        out_shape=(
            jax.ShapeDtypeStruct(colour.shape, f32),
            jax.ShapeDtypeStruct(w_in.shape, f32),
            jax.ShapeDtypeStruct(w_mid.shape, f32),
            jax.ShapeDtypeStruct(w_out.shape, f32),
        ),
        in_specs=[pl.BlockSpec(memory_space=vmem)] * 3,
        out_specs=[pl.BlockSpec(memory_space=vmem)] * 4,
        name="widen",
    )(colour, grads.reshape(2 * owned, hid, hid), grad_out)


def solution(mesh):
    in_specs = (
        P(None, ("region", "replica"), None),
        P(("region", "replica"), None),
        P(None, ("region", "replica")),
        P(("region", "replica"), None, None),
        P(("region", "replica"), None),
        P(),
        P("region", None, None),
        P("region", None, None),
        P("region", None, None),
    )
    out_specs = (
        P(None, ("region", "replica")),
        P("region", None, None),
        P("region", None, None),
        P("region", None, None),
    )
    return jax.shard_map(
        on_device, mesh=mesh, in_specs=in_specs, out_specs=out_specs, check_vma=False
    )
```

```python
import functools

import jax
import jax.numpy as jnp
from jax import lax
from jax.experimental import pallas as pl
from jax.experimental.pallas import tpu as pltpu
from jax.sharding import PartitionSpec as P

MESH = pl.DeviceIdType.MESH
f32, bf16 = jnp.float32, jnp.bfloat16
LANES = 128
ROW = 16
loss_scale = 16.0

SIN_HALF = (4.442882919048677, -7.308245676836255, 3.606354025126868, -0.8461104138552027, 0.10982204430121903)
COS_HALF = (1.4142134959439656, -6.978850908781684, 5.739459581977078, -1.8835528214703008, 0.31067786282805515)


def iota(shape, dim):
    return lax.broadcasted_iota(jnp.int32, shape, dim)


def dot(a, b):
    return jnp.dot(a, b, preferred_element_type=f32)


def dot_nt(a, b):
    return lax.dot_general(a, b, (((1,), (1,)), ((), ())), preferred_element_type=f32)


def dot_tn(a, b):
    return lax.dot_general(a, b, (((0,), (0,)), ((), ())), preferred_element_type=f32)


def split(x):
    high = x.astype(bf16).astype(f32)
    rest = x - high
    middle = rest.astype(bf16).astype(f32)
    return high, middle, rest - middle


def wide(x):
    return jnp.concatenate(split(x), 1).astype(bf16)


def tall(x):
    return jnp.concatenate((*split(x), jnp.zeros_like(x)), 0).astype(bf16)


def unwide(x):
    w = x.shape[1] // 3
    return x[:, :w] + x[:, w : 2 * w] + x[:, 2 * w :]


def untall(x):
    w = x.shape[0] // 4
    return x[:w] + x[w : 2 * w] + x[2 * w : 3 * w]


def polynomial(coefficients, z):
    value = jnp.full_like(z, coefficients[-1])
    for coefficient in coefficients[-2::-1]:
        value = value * z + coefficient
    return value


def sin_cos_turns(turns):
    rest = turns - jnp.round(turns)
    square = rest * rest
    s = polynomial(SIN_HALF, square) * rest
    c = polynomial(COS_HALF, square)
    return s * c, 1.0 - s * s


def column_from_row(eye, row):
    return jnp.sum(jnp.where(eye, jnp.broadcast_to(row, eye.shape), 0.0), axis=1, keepdims=True)


def on_lanes(x, width=LANES):
    return jnp.concatenate([x, jnp.zeros((x.shape[0], width - x.shape[1]), x.dtype)], 1)


def exchange_start(count, me, axis, source_of, target, send, recv):
    def start(k, carry):
        peer = lax.rem(me + k, count)
        pltpu.make_async_remote_copy(
            src_ref=source_of(peer),
            dst_ref=target.at[me],
            send_sem=send.at[k],
            recv_sem=recv.at[k],
            device_id={axis: peer},
            device_id_type=MESH,
        ).start()
        return carry

    lax.fori_loop(1, count, start, 0)


def exchange_wait(count, me, axis, source_of, target, send, recv, sides=("recv", "send")):
    def wait(k, carry):
        peer = lax.rem(me + k, count)
        origin = lax.rem(me + count - k, count)
        copy = pltpu.make_async_remote_copy(
            src_ref=source_of(peer),
            dst_ref=target.at[origin],
            send_sem=send.at[k],
            recv_sem=recv.at[k],
            device_id={axis: peer},
            device_id_type=MESH,
        )
        if "recv" in sides:
            copy.wait_recv()
        if "send" in sides:
            copy.wait_send()
        return carry

    lax.fori_loop(1, count, wait, 0)


def step_kernel(
    n, m, cap, segs, seg_len,
    pos_ref, gap_ref, tgt_ref, reg_ref, rank_ref, freq_ref, w_out_ref, w_in_hbm, w_mid_hbm,
    colour_ref, grads_ref, grad_out_ref,
    send_a, recv_a, send_b, recv_b, send_c, recv_c,
    feat, hid_one, hid_two, raw, shade, alpha, gaps, raw_grad, grad_two, feat_t, one_t,
    place, phase_hi, phase_lo, slots_x, w_in, w_mid, wb_in, wb_mid, wb_out, wb_out_t,
    acc, acc_out, part, part_recv, out_send, out_recv,
    sem_w, sem_a, sem_b, sem_c, sem_rs, sem_ag, sem_go,
):
    me = lax.axis_index("region")
    mez = lax.axis_index("replica")
    owned = w_in.shape[0]
    rays = pos_ref.shape[1]
    seg_dev = rays * segs
    slots = n * cap
    chunks = seg_len // 2
    per_tile = LANES // ROW
    half_lanes = LANES // 2

    barrier = pltpu.get_barrier_semaphore()

    def greet_region(k, carry):
        pl.semaphore_signal(
            barrier, inc=1, device_id={"region": lax.rem(me + k, n)}, device_id_type=MESH
        )
        return carry

    def greet_replica(k, carry):
        pl.semaphore_signal(
            barrier, inc=1, device_id={"replica": lax.rem(mez + k, m)}, device_id_type=MESH
        )
        return carry

    lax.fori_loop(1, n, greet_region, 0)
    lax.fori_loop(1, m, greet_replica, 0)
    load_in = pltpu.make_async_copy(w_in_hbm, w_in, sem_w.at[0])
    load_mid = pltpu.make_async_copy(w_mid_hbm, w_mid, sem_w.at[1])
    load_in.start()
    load_mid.start()

    eye = iota((rays, rays), 0) == iota((rays, rays), 1)
    region_col = jnp.concatenate([column_from_row(eye, reg_ref[s].astype(f32)) for s in range(segs)], 0)
    lane = iota((seg_dev, LANES), 1)
    onehot = jnp.where(region_col == lane.astype(f32), 1.0, 0.0)
    before = jnp.where(iota((seg_dev, seg_dev), 0) > iota((seg_dev, seg_dev), 1), 1.0, 0.0)
    earlier = dot(before.astype(bf16), onehot.astype(bf16))
    order_col = jnp.sum(earlier * onehot, axis=1, keepdims=True)
    owner_col = jnp.floor((region_col + 0.5) * (1.0 / owned))
    local_col = region_col - owned * owner_col
    keys = jnp.where(lane == 0, owner_col * ROW + order_col, jnp.where(lane == 1, owner_col, 0.0)).T
    slot_row, owner_row = keys[0:1, :], keys[1:2, :]

    pieces = []
    lane_s = iota((rays, LANES), 1) & (half_lanes - 1)
    for s in range(segs):
        packed = jnp.zeros((rays, LANES), f32)
        for d in range(4):
            source = on_lanes(pos_ref[d] if d < 3 else gap_ref[...].astype(f32))
            shift = seg_len * (d - s)
            moved = pltpu.roll(source, shift % LANES, 1)
            packed = jnp.where((lane_s >= seg_len * d) & (lane_s < seg_len * (d + 1)), moved, packed)
        pieces.append(packed[:, :])
    packed = jnp.concatenate(pieces, 0)
    packed = jnp.where(lane < half_lanes, packed, pltpu.roll(packed, half_lanes, 1))
    own_half = (lane >= half_lanes).astype(f32) == local_col
    packed = wide(jnp.where(own_half, packed, 0.0))
    scatter = jnp.where(iota((n * ROW, seg_dev), 0).astype(f32) == slot_row, 1.0, 0.0).astype(bf16)
    send_a[...] = unwide(dot(scatter, packed)).reshape(send_a.shape)

    pl.semaphore_wait(barrier, n - 1 + m - 1)
    exchange_a = (n, me, "region", lambda p: send_a.at[p], recv_a, sem_a.at[0], sem_a.at[1])
    exchange_start(*exchange_a)
    recv_a[me] = send_a[me]

    slot_id = iota((slots, 1), 0).astype(f32)
    peer_id = jnp.floor((slot_id + 0.5) * (1.0 / cap))
    spot = slot_id + (ROW - cap) * peer_id
    place[...] = jnp.where(iota((slots, n * ROW), 1).astype(f32) == spot, 1.0, 0.0).astype(bf16)
    freq_high, freq_middle, freq_low = split(freq_ref[...])
    width = freq_ref.shape[1]

    def spread(values):
        return jnp.concatenate([jnp.broadcast_to(values[d : d + 1], (seg_len, width)) for d in range(3)], 0)

    rest16 = jnp.zeros((seg_len, width), f32)
    rest32 = jnp.zeros((2 * seg_len, width), f32)
    table_hi = jnp.concatenate(
        [spread(freq_high), spread(freq_high), rest32, spread(freq_high), rest16, spread(freq_middle), rest16], 0
    )
    table_lo = jnp.concatenate([spread(freq_low), spread(freq_middle), rest32], 0)
    for i in range(seg_len):
        cols = slice((i % 2) * width, (i % 2 + 1) * width)
        mine = (iota(table_hi.shape, 0) & (seg_len - 1)) == i
        phase_hi[i // 2, :, cols] = jnp.where(mine, table_hi, 0.0).astype(bf16)
        mine = (iota(table_lo.shape, 0) & (seg_len - 1)) == i
        phase_lo[i // 2, :, cols] = jnp.where(mine, table_lo, 0.0).astype(bf16)
    load_in.wait()
    load_mid.wait()
    for l in range(owned):
        wb_in[l] = w_in[l].astype(bf16)
        wb_mid[l] = w_mid[l].astype(bf16)
        out_rows = jnp.concatenate([w_out_ref[l], jnp.zeros((LANES - 4, w_out_ref.shape[2]), f32)], 0)
        wb_out[l] = out_rows[:8].astype(bf16)
        wb_out_t[l] = out_rows.T.astype(bf16)

    exchange_wait(*exchange_a, ("recv",))

    high, middle, low = split(recv_a[...].reshape(n * ROW, LANES))
    lane_r = iota(high.shape, 1)
    coords = 3 * seg_len
    high_turned = pltpu.roll(high, half_lanes, 1)
    pick_gap = jnp.where(
        iota((seg_len, 2 * LANES), 1) == iota((seg_len, 2 * LANES), 0) + LANES + coords, 1.0, 0.0
    ).astype(bf16)
    for l in range(owned):
        own, other = (high, high_turned) if l == 0 else (high_turned, high)
        tail = low if l == 0 else pltpu.roll(low, half_lanes, 1)
        first = jnp.where(lane_r < coords, own, pltpu.roll(middle, coords + l * half_lanes, 1))
        second = jnp.where(lane_r < coords, tail, jnp.where(lane_r < half_lanes, own, other))
        slots_x[l] = dot(place[...], jnp.concatenate([first, second], 1).astype(bf16)).astype(bf16)
        gaps[l] = dot_nt(pick_gap, slots_x[l])

    def phases(l, c):
        return dot(slots_x[l], phase_hi[c]) + dot(slots_x[l][:, :LANES], phase_lo[c])

    def encode(l, c, turns):
        sines, cosines = sin_cos_turns(turns)
        for j in range(2):
            cols = slice(j * width, (j + 1) * width)
            feat[l, c, j * slots : (j + 1) * slots, :] = jnp.concatenate(
                [sines[:, cols], cosines[:, cols]], 1
            ).astype(bf16)

    def render(l):
        depth = jnp.zeros((8, slots), f32)
        clear = jnp.ones((8, slots), f32)
        colour = jnp.zeros((8, slots), f32)
        for i in range(seg_len):
            value = raw[l, i // 2][:, (i % 2) * slots : (i % 2 + 1) * slots]
            density = jnp.broadcast_to(value[0:1], value.shape)
            density = jnp.maximum(density, 0.0) + jnp.log1p(jnp.exp(-jnp.abs(density)))
            emitted = 1.0 / (1.0 + jnp.exp(-value))
            depth = depth + density * gaps[l][i : i + 1]
            after = jnp.exp(-depth)
            colour = colour + (clear - after) * emitted
            clear = after
            shade[l, i] = emitted
            alpha[l, i] = after
        return jnp.where(sub == 0, clear, colour)[:4]

    sub = iota((8, slots), 0)
    steps = [(l, c) for c in range(chunks) for l in range(owned)]
    encode(*steps[0], phases(*steps[0]))
    rendered = []
    for at, (l, c) in enumerate(steps):
        ahead = steps[at + 1] if at + 1 < len(steps) else None
        if ahead:
            turns = phases(*ahead)
        one = jnp.maximum(dot(feat[l, c], wb_in[l]), 0.0).astype(bf16)
        hid_one[l, c] = one
        if ahead:
            encode(*ahead, turns)
        two = jnp.maximum(dot(one, wb_mid[l]), 0.0).astype(bf16)
        hid_two[l, c] = two
        raw[l, c] = dot(two, wb_out_t[l]).T[:8]
        if c == chunks - 1:
            rendered.append(render(l))
    returned = untall(dot(tall(jnp.concatenate(rendered, 0)), place[...]))
    for q in range(send_b.shape[0]):
        send_b[q] = returned[:, q * LANES : (q + 1) * LANES]

    exchange_b = (n, me, "region", lambda p: send_b.at[p // per_tile], recv_b, sem_b.at[0], sem_b.at[1])
    exchange_start(*exchange_b)
    recv_b[me] = send_b[me // per_tile]

    unit_mask = ((lane & (ROW - 1)).astype(f32) == order_col) & own_half
    channel = (lane // ROW) & 3
    owner_mask = jnp.where(iota((seg_dev, n), 1).astype(f32) == owner_col, 1.0, 0.0).astype(bf16)
    owner_turned = jnp.where(iota((n, seg_dev), 0).astype(f32) == owner_row, 1.0, 0.0).astype(bf16)
    rank = [column_from_row(eye, rank_ref[s : s + 1, :].astype(f32)) for s in range(segs)]
    earlier_than = [[rank[t] < rank[s] for t in range(segs)] for s in range(segs)]
    target = [column_from_row(eye, tgt_ref[c : c + 1, :]) for c in range(3)]
    shift_home = lax.rem(me, per_tile) * ROW

    for l in range(owned):
        for c in range(chunks):
            one_t[l, c] = hid_one[l, c].T

    exchange_wait(*exchange_b, ("recv",))

    lane_n = iota((n, LANES), 1)
    mine = jnp.zeros((n, LANES), f32)
    for ch in range(8):
        moved = pltpu.roll(recv_b[:, ch, :], lax.rem(ch * ROW - shift_home + LANES, LANES), 1)
        mine = jnp.where((lane_n >= ch * ROW) & (lane_n < (ch + 1) * ROW), moved, mine)
    found = jnp.where(unit_mask, unwide(dot(owner_mask, wide(mine))), 0.0)
    columns = [jnp.sum(jnp.where(channel == ch, found, 0.0), axis=1, keepdims=True) for ch in range(4)]
    by_seg = [[col[s * rays : (s + 1) * rays] for s in range(segs)] for col in columns]
    trans, colours = by_seg[0], by_seg[1:]

    def front(s, skip):
        product = jnp.ones((rays, 1), f32)
        for t in range(segs):
            if t not in skip:
                product = product * jnp.where(earlier_than[s][t], trans[t], 1.0)
        return product

    prefix = [front(s, (s,)) for s in range(segs)]
    pulled = []
    for c in range(3):
        total = colours[c][0] * prefix[0]
        for s in range(1, segs):
            total = total + colours[c][s] * prefix[s]
        colour_ref[c : c + 1, :] = jnp.sum(
            jnp.where(eye, jnp.broadcast_to(total, eye.shape), 0.0), axis=0, keepdims=True
        )
        pulled.append((2.0 * loss_scale) * (total - target[c]))
    weight = [
        pulled[0] * colours[0][s] + pulled[1] * colours[1][s] + pulled[2] * colours[2][s] for s in range(segs)
    ]
    back = [[], [], [], []]
    for t in range(segs):
        total = jnp.zeros((rays, 1), f32)
        for s in range(segs):
            if s != t:
                total = total + jnp.where(earlier_than[s][t], weight[s] * front(s, (s, t)), 0.0)
        back[0].append(total)
        for c in range(3):
            back[c + 1].append(pulled[c] * prefix[t])
    spread_back = jnp.zeros((seg_dev, LANES), f32)
    for ch in range(4):
        spread_back = jnp.where(channel == ch, jnp.concatenate(back[ch], 0), spread_back)
    spread_back = jnp.where(unit_mask, spread_back, 0.0)
    homeward = unwide(dot(owner_turned, wide(spread_back)))
    for ch in range(8):
        moved = pltpu.roll(homeward, lax.rem(shift_home - ch * ROW + LANES, LANES), 1)
        send_c[:, ch, :] = jnp.where((lane_n >= shift_home) & (lane_n < shift_home + ROW), moved, 0.0)

    exchange_c = (n, me, "region", lambda p: send_c.at[p], recv_c, sem_c.at[0], sem_c.at[1])
    exchange_start(*exchange_c)
    recv_c[me] = send_c[me]
    for l in range(owned):
        for c in range(chunks):
            feat_t[l, c] = feat[l, c].T
    exchange_wait(*exchange_c, ("recv",))

    groups = []
    for q in range(send_b.shape[0]):
        total = recv_c[q * per_tile]
        for k in range(1, per_tile):
            total = total + recv_c[q * per_tile + k]
        groups.append(total)
    cotangent = untall(dot_nt(tall(jnp.concatenate(groups, 1)), place[...]))

    def render_back(l):
        pull = cotangent if l == 0 else pltpu.roll(cotangent, 4, 0)
        later = pull[0:1] * alpha[l, seg_len - 1][0:1]
        for i in range(seg_len - 1, -1, -1):
            emitted = shade[l, i]
            after = alpha[l, i]
            ahead = alpha[l, i - 1] if i > 0 else jnp.ones_like(after)
            share = ahead - after
            lit = pull * emitted
            lit = jnp.sum(jnp.where((sub >= 1) & (sub <= 3), lit, 0.0), axis=0, keepdims=True)
            later = later + lit * share[0:1]
            density = (lit * ahead[0:1] - later) * gaps[l][i : i + 1] * emitted[0:1]
            tint = pull * share * emitted * (1.0 - emitted)
            values = jnp.where(sub == 0, density, jnp.where(sub <= 3, tint, 0.0))
            raw_grad[l, i // 2, :, (i % 2) * slots : (i % 2 + 1) * slots] = tall(values)

    def exchange_r(p):
        return (m, mez, "replica", lambda z: part.at[p, z], part_recv.at[p], sem_rs.at[p, 0], sem_rs.at[p, 1])

    def exchange_g(p):
        return (m, mez, "replica", lambda z: grads_ref.at[p, mez], grads_ref.at[p], sem_ag.at[p, 0], sem_ag.at[p, 1])

    def send_part(p):
        part[p] = acc[...].astype(bf16).reshape(part.shape[1:])
        exchange_start(*exchange_r(p))

    def sum_part(p):
        part_recv[p, mez] = part[p, mez]
        exchange_wait(*exchange_r(p))
        total = part_recv[p, 0].astype(f32)
        for k in range(1, m):
            total = total + part_recv[p, k].astype(f32)
        grads_ref[p, mez] = total.astype(bf16)

    two_steps = m == 8
    last = 2 * owned - 1

    def hop(p, k, chunk, target):
        return pltpu.make_async_remote_copy(
            src_ref=grads_ref.at[p, chunk],
            dst_ref=grads_ref.at[p, chunk],
            send_sem=sem_ag.at[p, 0, k],
            recv_sem=sem_ag.at[p, 1, k],
            device_id={"replica": target},
            device_id_type=MESH,
        )

    def away(distance):
        return lax.rem(mez + distance + m, m)

    side = 2 - 4 * lax.rem(mez, 2)
    near = ((0, 1), (1, -1), (2, 2), (3, -2))
    far = ((4, away(-2), away(1)), (5, away(2), away(-1)), (6, away(-side), away(side)))

    def gather_near(p):
        if p == last or not two_steps:
            exchange_start(*exchange_g(p))
            return
        for k, distance in near:
            hop(p, k, mez, away(distance)).start()

    def gather_far(p):
        if p == last or not two_steps:
            return
        for k, distance in near[2:]:
            hop(p, k, away(-distance), away(distance)).wait_recv()
        for k, chunk, target in far:
            hop(p, k, chunk, target).start()

    def gather_wait(p):
        if p == last or not two_steps:
            exchange_wait(*exchange_g(p))
            return
        for k, distance in near[:2]:
            hop(p, k, away(-distance), away(distance)).wait_recv()
        for k, distance in ((4, -3), (5, 3), (6, 4)):
            hop(p, k, away(distance), away(1)).wait_recv()
        for k, distance in near:
            hop(p, k, mez, away(distance)).wait_send()
        for k, chunk, target in far:
            hop(p, k, chunk, target).wait_send()

    for l in range(owned):
        render_back(l)
        head = jnp.concatenate([wb_out[l].astype(f32)] * 4, 0).astype(bf16)

        def second_grad(c):
            grad_two[l, c] = jnp.where(hid_two[l, c] > 0, dot_tn(raw_grad[l, c], head), 0.0).astype(bf16)

        def first_grad(c):
            return jnp.where(hid_one[l, c] > 0, dot_nt(grad_two[l, c], wb_mid[l]), 0.0).astype(bf16)

        second_grad(0)
        for c in range(chunks):
            if c + 1 < chunks:
                second_grad(c + 1)
            term = dot(one_t[l, c], grad_two[l, c])
            acc[...] = term if c == 0 else acc[...] + term
        send_part(2 * l)
        if l > 0:
            sum_part(2 * l - 2)
            gather_near(2 * l - 2)
        now = first_grad(0)
        for c in range(chunks):
            later = first_grad(c + 1) if c + 1 < chunks else None
            term = dot(feat_t[l, c], now)
            acc[...] = term if c == 0 else acc[...] + term
            now = later
        send_part(2 * l + 1)

    sum_part(1)
    gather_near(1)

    half = hid_two.shape[3] // 2
    sums = []
    for l in range(owned):
        for c in range(chunks):
            term = dot(raw_grad[l, c], hid_two[l, c])
            acc_out[...] = term if c == 0 else acc_out[...] + term
        summed = untall(acc_out[...])[:4]
        sums += [summed[:, :half], summed[:, half:]]
    out_send[...] = jnp.concatenate(sums, 0).astype(bf16)
    exchange_o = (m, mez, "replica", lambda z: out_send, out_recv, sem_go.at[0], sem_go.at[1])
    exchange_start(*exchange_o)
    out_recv[mez] = out_send[...]

    sum_part(2)
    gather_near(2)
    gather_far(0)
    gather_far(1)
    sum_part(last)
    gather_near(last)
    gather_far(2)
    for exchange in (exchange_a, exchange_b, exchange_c):
        exchange_wait(*exchange, ("send",))
    exchange_wait(*exchange_o)
    total = out_recv[0].astype(f32)
    for k in range(1, m):
        total = total + out_recv[k].astype(f32)
    for l in range(owned):
        grad_out_ref[l] = jnp.concatenate([total[8 * l : 8 * l + 4], total[8 * l + 4 : 8 * l + 8]], 1)
    for p in range(2 * owned):
        gather_wait(p)


def finish_kernel(colour, grads, grad_out, colour_ref, grad_in_ref, grad_mid_ref, grad_out_ref):
    colour_ref[...] = colour[...]
    grad_out_ref[...] = grad_out[...]
    for l in range(grad_in_ref.shape[0]):
        grad_mid_ref[l] = grads[2 * l].astype(f32)
        grad_in_ref[l] = grads[2 * l + 1].astype(f32)


def on_device(positions, spacing, targets, seg_region, seg_rank, frequencies, w_in, w_mid, w_out):
    n, m = lax.axis_size("region"), lax.axis_size("replica")
    rays, segs = seg_rank.shape
    seg_len = positions.shape[2] // segs
    owned, enc, hid = w_in.shape
    cap = 3 * rays * segs // (owned * n)
    slots, chunk = n * cap, 2 * n * cap
    chunks = seg_len // 2
    groups = n * ROW // LANES
    deep = hid // m
    half = w_out.shape[2] // 2
    vmem = pltpu.VMEM
    semaphores = pltpu.SemaphoreType.DMA
    colour, grads, grad_out = pl.pallas_call(
        functools.partial(step_kernel, n, m, cap, segs, seg_len),
        out_shape=(
            jax.ShapeDtypeStruct((3, rays), f32),
            jax.ShapeDtypeStruct((2 * owned, m, deep, hid), bf16),
            jax.ShapeDtypeStruct(w_out.shape, f32),
        ),
        in_specs=[pl.BlockSpec(memory_space=vmem)] * 7 + [pl.BlockSpec(memory_space=pl.ANY)] * 2,
        out_specs=[pl.BlockSpec(memory_space=vmem)] * 3,
        scratch_shapes=[
            vmem((n, ROW, LANES), f32),
            vmem((n, ROW, LANES), f32),
            vmem((groups, 8, LANES), f32),
            vmem((n, 8, LANES), f32),
            vmem((n, 8, LANES), f32),
            vmem((n, 8, LANES), f32),
            vmem((owned, chunks, chunk, enc), bf16),
            vmem((owned, chunks, chunk, hid), bf16),
            vmem((owned, chunks, chunk, hid), bf16),
            vmem((owned, chunks, 8, chunk), f32),
            vmem((owned, seg_len, 8, slots), f32),
            vmem((owned, seg_len, 8, slots), f32),
            vmem((owned, seg_len, slots), f32),
            vmem((owned, chunks, 32, chunk), bf16),
            vmem((owned, chunks, chunk, hid), bf16),
            vmem((owned, chunks, enc, chunk), bf16),
            vmem((owned, chunks, hid, chunk), bf16),
            vmem((slots, n * ROW), bf16),
            vmem((chunks, 2 * LANES, enc), bf16),
            vmem((chunks, LANES, enc), bf16),
            vmem((owned, slots, 2 * LANES), bf16),
            vmem((owned, enc, hid), f32),
            vmem((owned, hid, hid), f32),
            vmem((owned, enc, hid), bf16),
            vmem((owned, hid, hid), bf16),
            vmem((owned, 8, hid), bf16),
            vmem((owned, hid, LANES), bf16),
            vmem((hid, hid), f32),
            vmem((32, hid), f32),
            vmem((2 * owned, m, deep, hid), bf16),
            vmem((2 * owned, m, deep, hid), bf16),
            vmem((8 * owned, half), bf16),
            vmem((m, 8 * owned, half), bf16),
            semaphores((2,)),
            semaphores((2, n)),
            semaphores((2, n)),
            semaphores((2, n)),
            semaphores((2 * owned, 2, m)),
            semaphores((2 * owned, 2, m)),
            semaphores((2, m)),
        ],
        compiler_params=pltpu.CompilerParams(
            collective_id=0, has_side_effects=True, vmem_limit_bytes=56 * 2**20
        ),
        name="radiance_step",
    )(
        positions, spacing, targets, seg_region.transpose(1, 2, 0), seg_rank.T, frequencies, w_out, w_in, w_mid
    )
    return pl.pallas_call(
        finish_kernel,
        out_shape=(
            jax.ShapeDtypeStruct(colour.shape, f32),
            jax.ShapeDtypeStruct(w_in.shape, f32),
            jax.ShapeDtypeStruct(w_mid.shape, f32),
            jax.ShapeDtypeStruct(w_out.shape, f32),
        ),
        in_specs=[pl.BlockSpec(memory_space=vmem)] * 3,
        out_specs=[pl.BlockSpec(memory_space=vmem)] * 4,
        name="widen",
    )(colour, grads.reshape(2 * owned, hid, hid), grad_out)


def solution(mesh):
    in_specs = (
        P(None, ("region", "replica"), None),
        P(("region", "replica"), None),
        P(None, ("region", "replica")),
        P(("region", "replica"), None, None),
        P(("region", "replica"), None),
        P(),
        P("region", None, None),
        P("region", None, None),
        P("region", None, None),
    )
    out_specs = (
        P(None, ("region", "replica")),
        P("region", None, None),
        P("region", None, None),
        P("region", None, None),
    )
    return jax.shard_map(
        on_device, mesh=mesh, in_specs=in_specs, out_specs=out_specs, check_vma=False
    )
```

```python
import functools

import jax
import jax.numpy as jnp
from jax import lax
from jax.experimental import pallas as pl
from jax.experimental.pallas import tpu as pltpu
from jax.sharding import PartitionSpec as P

MESH = pl.DeviceIdType.MESH
f32, bf16 = jnp.float32, jnp.bfloat16
LANES = 128
ROW = 16
loss_scale = 16.0

SIN_HALF = (4.442882919048677, -7.308245676836255, 3.606354025126868, -0.8461104138552027, 0.10982204430121903)
COS_HALF = (1.4142134959439656, -6.978850908781684, 5.739459581977078, -1.8835528214703008, 0.31067786282805515)


def iota(shape, dim):
    return lax.broadcasted_iota(jnp.int32, shape, dim)


def dot(a, b):
    return jnp.dot(a, b, preferred_element_type=f32)


def dot_nt(a, b):
    return lax.dot_general(a, b, (((1,), (1,)), ((), ())), preferred_element_type=f32)


def dot_tn(a, b):
    return lax.dot_general(a, b, (((0,), (0,)), ((), ())), preferred_element_type=f32)


def split(x):
    high = x.astype(bf16).astype(f32)
    rest = x - high
    middle = rest.astype(bf16).astype(f32)
    return high, middle, rest - middle


def wide(x):
    return jnp.concatenate(split(x), 1).astype(bf16)


def tall(x):
    return jnp.concatenate((*split(x), jnp.zeros_like(x)), 0).astype(bf16)


def unwide(x):
    w = x.shape[1] // 3
    return x[:, :w] + x[:, w : 2 * w] + x[:, 2 * w :]


def untall(x):
    w = x.shape[0] // 4
    return x[:w] + x[w : 2 * w] + x[2 * w : 3 * w]


def polynomial(coefficients, z):
    value = jnp.full_like(z, coefficients[-1])
    for coefficient in coefficients[-2::-1]:
        value = value * z + coefficient
    return value


def sin_cos_turns(turns):
    rest = turns - jnp.round(turns)
    square = rest * rest
    s = polynomial(SIN_HALF, square) * rest
    c = polynomial(COS_HALF, square)
    return s * c, 1.0 - s * s


def column_from_row(eye, row):
    return jnp.sum(jnp.where(eye, jnp.broadcast_to(row, eye.shape), 0.0), axis=1, keepdims=True)


def on_lanes(x, width=LANES):
    return jnp.concatenate([x, jnp.zeros((x.shape[0], width - x.shape[1]), x.dtype)], 1)


def exchange_start(count, me, axis, source_of, target, send, recv):
    def start(k, carry):
        peer = lax.rem(me + k, count)
        pltpu.make_async_remote_copy(
            src_ref=source_of(peer),
            dst_ref=target.at[me],
            send_sem=send.at[k],
            recv_sem=recv.at[k],
            device_id={axis: peer},
            device_id_type=MESH,
        ).start()
        return carry

    lax.fori_loop(1, count, start, 0)


def exchange_wait(count, me, axis, source_of, target, send, recv, sides=("recv", "send")):
    def wait(k, carry):
        peer = lax.rem(me + k, count)
        origin = lax.rem(me + count - k, count)
        copy = pltpu.make_async_remote_copy(
            src_ref=source_of(peer),
            dst_ref=target.at[origin],
            send_sem=send.at[k],
            recv_sem=recv.at[k],
            device_id={axis: peer},
            device_id_type=MESH,
        )
        if "recv" in sides:
            copy.wait_recv()
        if "send" in sides:
            copy.wait_send()
        return carry

    lax.fori_loop(1, count, wait, 0)


def step_kernel(
    n, m, cap, segs, seg_len,
    pos_ref, gap_ref, tgt_ref, reg_ref, rank_ref, freq_ref, w_out_ref, w_in_hbm, w_mid_hbm,
    colour_ref, grads_ref, grad_out_ref,
    send_a, recv_a, send_b, recv_b, send_c, recv_c,
    feat, hid_one, hid_two, raw, shade, alpha, gaps, raw_grad, grad_two, feat_t, one_t,
    place, phase_hi, phase_lo, slots_x, w_in, w_mid, wb_in, wb_mid, wb_out, wb_out_t,
    acc, acc_out, part, part_recv, out_send, out_recv,
    sem_w, sem_a, sem_b, sem_c, sem_rs, sem_ag, sem_go,
):
    me = lax.axis_index("region")
    mez = lax.axis_index("replica")
    owned = w_in.shape[0]
    rays = pos_ref.shape[1]
    seg_dev = rays * segs
    slots = n * cap
    chunks = seg_len // 2
    per_tile = LANES // ROW
    half_lanes = LANES // 2

    barrier = pltpu.get_barrier_semaphore()

    def greet_region(k, carry):
        pl.semaphore_signal(
            barrier, inc=1, device_id={"region": lax.rem(me + k, n)}, device_id_type=MESH
        )
        return carry

    def greet_replica(k, carry):
        pl.semaphore_signal(
            barrier, inc=1, device_id={"replica": lax.rem(mez + k, m)}, device_id_type=MESH
        )
        return carry

    lax.fori_loop(1, n, greet_region, 0)
    lax.fori_loop(1, m, greet_replica, 0)
    load_in = pltpu.make_async_copy(w_in_hbm, w_in, sem_w.at[0])
    load_mid = pltpu.make_async_copy(w_mid_hbm, w_mid, sem_w.at[1])
    load_in.start()
    load_mid.start()

    eye = iota((rays, rays), 0) == iota((rays, rays), 1)
    region_col = jnp.concatenate([column_from_row(eye, reg_ref[s].astype(f32)) for s in range(segs)], 0)
    lane = iota((seg_dev, LANES), 1)
    onehot = jnp.where(region_col == lane.astype(f32), 1.0, 0.0)
    before = jnp.where(iota((seg_dev, seg_dev), 0) > iota((seg_dev, seg_dev), 1), 1.0, 0.0)
    earlier = dot(before.astype(bf16), onehot.astype(bf16))
    order_col = jnp.sum(earlier * onehot, axis=1, keepdims=True)
    owner_col = jnp.floor((region_col + 0.5) * (1.0 / owned))
    local_col = region_col - owned * owner_col
    keys = jnp.where(lane == 0, owner_col * ROW + order_col, jnp.where(lane == 1, owner_col, 0.0)).T
    slot_row, owner_row = keys[0:1, :], keys[1:2, :]

    pieces = []
    lane_s = iota((rays, LANES), 1) & (half_lanes - 1)
    for s in range(segs):
        packed = jnp.zeros((rays, LANES), f32)
        for d in range(4):
            source = on_lanes(pos_ref[d] if d < 3 else gap_ref[...].astype(f32))
            shift = seg_len * (d - s)
            moved = pltpu.roll(source, shift % LANES, 1)
            packed = jnp.where((lane_s >= seg_len * d) & (lane_s < seg_len * (d + 1)), moved, packed)
        pieces.append(packed[:, :])
    packed = jnp.concatenate(pieces, 0)
    packed = jnp.where(lane < half_lanes, packed, pltpu.roll(packed, half_lanes, 1))
    own_half = (lane >= half_lanes).astype(f32) == local_col
    packed = wide(jnp.where(own_half, packed, 0.0))
    scatter = jnp.where(iota((n * ROW, seg_dev), 0).astype(f32) == slot_row, 1.0, 0.0).astype(bf16)
    send_a[...] = unwide(dot(scatter, packed)).reshape(send_a.shape)

    pl.semaphore_wait(barrier, n - 1 + m - 1)
    exchange_a = (n, me, "region", lambda p: send_a.at[p], recv_a, sem_a.at[0], sem_a.at[1])
    exchange_start(*exchange_a)
    recv_a[me] = send_a[me]

    slot_id = iota((slots, 1), 0).astype(f32)
    peer_id = jnp.floor((slot_id + 0.5) * (1.0 / cap))
    spot = slot_id + (ROW - cap) * peer_id
    place[...] = jnp.where(iota((slots, n * ROW), 1).astype(f32) == spot, 1.0, 0.0).astype(bf16)
    freq_high, freq_middle, freq_low = split(freq_ref[...])
    width = freq_ref.shape[1]

    def spread(values):
        return jnp.concatenate([jnp.broadcast_to(values[d : d + 1], (seg_len, width)) for d in range(3)], 0)

    rest16 = jnp.zeros((seg_len, width), f32)
    rest32 = jnp.zeros((2 * seg_len, width), f32)
    table_hi = jnp.concatenate(
        [spread(freq_high), spread(freq_high), rest32, spread(freq_high), rest16, spread(freq_middle), rest16], 0
    )
    table_lo = jnp.concatenate([spread(freq_low), spread(freq_middle), rest32], 0)
    for i in range(seg_len):
        cols = slice((i % 2) * width, (i % 2 + 1) * width)
        mine = (iota(table_hi.shape, 0) & (seg_len - 1)) == i
        phase_hi[i // 2, :, cols] = jnp.where(mine, table_hi, 0.0).astype(bf16)
        mine = (iota(table_lo.shape, 0) & (seg_len - 1)) == i
        phase_lo[i // 2, :, cols] = jnp.where(mine, table_lo, 0.0).astype(bf16)
    load_in.wait()
    load_mid.wait()
    for l in range(owned):
        wb_in[l] = w_in[l].astype(bf16)
        wb_mid[l] = w_mid[l].astype(bf16)
        out_rows = jnp.concatenate([w_out_ref[l], jnp.zeros((LANES - 4, w_out_ref.shape[2]), f32)], 0)
        wb_out[l] = out_rows[:8].astype(bf16)
        wb_out_t[l] = out_rows.T.astype(bf16)

    exchange_wait(*exchange_a, ("recv",))

    high, middle, low = split(recv_a[...].reshape(n * ROW, LANES))
    lane_r = iota(high.shape, 1)
    coords = 3 * seg_len
    high_turned = pltpu.roll(high, half_lanes, 1)
    pick_gap = jnp.where(
        iota((seg_len, 2 * LANES), 1) == iota((seg_len, 2 * LANES), 0) + LANES + coords, 1.0, 0.0
    ).astype(bf16)
    for l in range(owned):
        own, other = (high, high_turned) if l == 0 else (high_turned, high)
        tail = low if l == 0 else pltpu.roll(low, half_lanes, 1)
        first = jnp.where(lane_r < coords, own, pltpu.roll(middle, coords + l * half_lanes, 1))
        second = jnp.where(lane_r < coords, tail, jnp.where(lane_r < half_lanes, own, other))
        slots_x[l] = dot(place[...], jnp.concatenate([first, second], 1).astype(bf16)).astype(bf16)
        gaps[l] = dot_nt(pick_gap, slots_x[l])

    def phases(l, c):
        return dot(slots_x[l], phase_hi[c]) + dot(slots_x[l][:, :LANES], phase_lo[c])

    def encode(l, c, turns):
        sines, cosines = sin_cos_turns(turns)
        for j in range(2):
            cols = slice(j * width, (j + 1) * width)
            feat[l, c, j * slots : (j + 1) * slots, :] = jnp.concatenate(
                [sines[:, cols], cosines[:, cols]], 1
            ).astype(bf16)

    def render(l):
        depth = jnp.zeros((8, slots), f32)
        clear = jnp.ones((8, slots), f32)
        colour = jnp.zeros((8, slots), f32)
        for i in range(seg_len):
            value = raw[l, i // 2][:, (i % 2) * slots : (i % 2 + 1) * slots]
            density = jnp.broadcast_to(value[0:1], value.shape)
            density = jnp.maximum(density, 0.0) + jnp.log1p(jnp.exp(-jnp.abs(density)))
            emitted = 1.0 / (1.0 + jnp.exp(-value))
            depth = depth + density * gaps[l][i : i + 1]
            after = jnp.exp(-depth)
            colour = colour + (clear - after) * emitted
            clear = after
            shade[l, i] = emitted
            alpha[l, i] = after
        return jnp.where(sub == 0, clear, colour)[:4]

    sub = iota((8, slots), 0)
    zero = jnp.zeros((), bf16)
    steps = [(l, c) for c in range(chunks) for l in range(owned)]
    encode(*steps[0], phases(*steps[0]))
    rendered = []
    for at, (l, c) in enumerate(steps):
        ahead = steps[at + 1] if at + 1 < len(steps) else None
        if ahead:
            turns = phases(*ahead)
        one = jnp.maximum(dot(feat[l, c], wb_in[l]).astype(bf16), zero)
        hid_one[l, c] = one
        if ahead:
            encode(*ahead, turns)
        two = jnp.maximum(dot(one, wb_mid[l]).astype(bf16), zero)
        hid_two[l, c] = two
        raw[l, c] = dot(two, wb_out_t[l]).T[:8]
        if c == chunks - 1:
            rendered.append(render(l))
    returned = untall(dot(tall(jnp.concatenate(rendered, 0)), place[...]))
    for q in range(send_b.shape[0]):
        send_b[q] = returned[:, q * LANES : (q + 1) * LANES]

    exchange_b = (n, me, "region", lambda p: send_b.at[p // per_tile], recv_b, sem_b.at[0], sem_b.at[1])
    exchange_start(*exchange_b)
    recv_b[me] = send_b[me // per_tile]

    unit_mask = ((lane & (ROW - 1)).astype(f32) == order_col) & own_half
    channel = (lane // ROW) & 3
    owner_mask = jnp.where(iota((seg_dev, n), 1).astype(f32) == owner_col, 1.0, 0.0).astype(bf16)
    owner_turned = jnp.where(iota((n, seg_dev), 0).astype(f32) == owner_row, 1.0, 0.0).astype(bf16)
    rank = [column_from_row(eye, rank_ref[s : s + 1, :].astype(f32)) for s in range(segs)]
    earlier_than = [[rank[t] < rank[s] for t in range(segs)] for s in range(segs)]
    target = [column_from_row(eye, tgt_ref[c : c + 1, :]) for c in range(3)]
    shift_home = lax.rem(me, per_tile) * ROW

    for l in range(owned):
        for c in range(chunks):
            one_t[l, c] = hid_one[l, c].T

    exchange_wait(*exchange_b, ("recv",))

    lane_n = iota((n, LANES), 1)
    mine = jnp.zeros((n, LANES), f32)
    for ch in range(8):
        moved = pltpu.roll(recv_b[:, ch, :], lax.rem(ch * ROW - shift_home + LANES, LANES), 1)
        mine = jnp.where((lane_n >= ch * ROW) & (lane_n < (ch + 1) * ROW), moved, mine)
    found = jnp.where(unit_mask, unwide(dot(owner_mask, wide(mine))), 0.0)
    columns = [jnp.sum(jnp.where(channel == ch, found, 0.0), axis=1, keepdims=True) for ch in range(4)]
    by_seg = [[col[s * rays : (s + 1) * rays] for s in range(segs)] for col in columns]
    trans, colours = by_seg[0], by_seg[1:]

    def front(s, skip):
        product = jnp.ones((rays, 1), f32)
        for t in range(segs):
            if t not in skip:
                product = product * jnp.where(earlier_than[s][t], trans[t], 1.0)
        return product

    prefix = [front(s, (s,)) for s in range(segs)]
    pulled = []
    for c in range(3):
        total = colours[c][0] * prefix[0]
        for s in range(1, segs):
            total = total + colours[c][s] * prefix[s]
        colour_ref[c : c + 1, :] = jnp.sum(
            jnp.where(eye, jnp.broadcast_to(total, eye.shape), 0.0), axis=0, keepdims=True
        )
        pulled.append((2.0 * loss_scale) * (total - target[c]))
    weight = [
        pulled[0] * colours[0][s] + pulled[1] * colours[1][s] + pulled[2] * colours[2][s] for s in range(segs)
    ]
    back = [[], [], [], []]
    for t in range(segs):
        total = jnp.zeros((rays, 1), f32)
        for s in range(segs):
            if s != t:
                total = total + jnp.where(earlier_than[s][t], weight[s] * front(s, (s, t)), 0.0)
        back[0].append(total)
        for c in range(3):
            back[c + 1].append(pulled[c] * prefix[t])
    spread_back = jnp.zeros((seg_dev, LANES), f32)
    for ch in range(4):
        spread_back = jnp.where(channel == ch, jnp.concatenate(back[ch], 0), spread_back)
    spread_back = jnp.where(unit_mask, spread_back, 0.0)
    homeward = unwide(dot(owner_turned, wide(spread_back)))
    for ch in range(8):
        moved = pltpu.roll(homeward, lax.rem(shift_home - ch * ROW + LANES, LANES), 1)
        send_c[:, ch, :] = jnp.where((lane_n >= shift_home) & (lane_n < shift_home + ROW), moved, 0.0)

    exchange_c = (n, me, "region", lambda p: send_c.at[p], recv_c, sem_c.at[0], sem_c.at[1])
    exchange_start(*exchange_c)
    recv_c[me] = send_c[me]
    for l in range(owned):
        for c in range(chunks):
            feat_t[l, c] = feat[l, c].T
    exchange_wait(*exchange_c, ("recv",))

    groups = []
    for q in range(send_b.shape[0]):
        total = recv_c[q * per_tile]
        for k in range(1, per_tile):
            total = total + recv_c[q * per_tile + k]
        groups.append(total)
    cotangent = untall(dot_nt(tall(jnp.concatenate(groups, 1)), place[...]))

    def render_back(l):
        pull = cotangent if l == 0 else pltpu.roll(cotangent, 4, 0)
        later = pull[0:1] * alpha[l, seg_len - 1][0:1]
        for i in range(seg_len - 1, -1, -1):
            emitted = shade[l, i]
            after = alpha[l, i]
            ahead = alpha[l, i - 1] if i > 0 else jnp.ones_like(after)
            share = ahead - after
            lit = pull * emitted
            lit = jnp.sum(jnp.where((sub >= 1) & (sub <= 3), lit, 0.0), axis=0, keepdims=True)
            later = later + lit * share[0:1]
            density = (lit * ahead[0:1] - later) * gaps[l][i : i + 1] * emitted[0:1]
            tint = pull * share * emitted * (1.0 - emitted)
            values = jnp.where(sub == 0, density, jnp.where(sub <= 3, tint, 0.0))
            raw_grad[l, i // 2, :, (i % 2) * slots : (i % 2 + 1) * slots] = tall(values)

    def exchange_r(p):
        return (m, mez, "replica", lambda z: part.at[p, z], part_recv.at[p], sem_rs.at[p, 0], sem_rs.at[p, 1])

    def exchange_g(p):
        return (m, mez, "replica", lambda z: grads_ref.at[p, mez], grads_ref.at[p], sem_ag.at[p, 0], sem_ag.at[p, 1])

    def send_part(p):
        part[p] = acc[...].astype(bf16).reshape(part.shape[1:])
        exchange_start(*exchange_r(p))

    def sum_part(p):
        part_recv[p, mez] = part[p, mez]
        exchange_wait(*exchange_r(p))
        total = part_recv[p, 0].astype(f32)
        for k in range(1, m):
            total = total + part_recv[p, k].astype(f32)
        grads_ref[p, mez] = total.astype(bf16)

    two_steps = m == 8
    last = 2 * owned - 1

    def hop(p, k, chunk, target):
        return pltpu.make_async_remote_copy(
            src_ref=grads_ref.at[p, chunk],
            dst_ref=grads_ref.at[p, chunk],
            send_sem=sem_ag.at[p, 0, k],
            recv_sem=sem_ag.at[p, 1, k],
            device_id={"replica": target},
            device_id_type=MESH,
        )

    def away(distance):
        return lax.rem(mez + distance + m, m)

    side = 2 - 4 * lax.rem(mez, 2)
    near = ((0, 1), (1, -1), (2, 2), (3, -2))
    far = ((4, away(-2), away(1)), (5, away(2), away(-1)), (6, away(-side), away(side)))

    def gather_near(p):
        if p == last or not two_steps:
            exchange_start(*exchange_g(p))
            return
        for k, distance in near:
            hop(p, k, mez, away(distance)).start()

    def gather_far(p):
        if p == last or not two_steps:
            return
        for k, distance in near[2:]:
            hop(p, k, away(-distance), away(distance)).wait_recv()
        for k, chunk, target in far:
            hop(p, k, chunk, target).start()

    def gather_wait(p):
        if p == last or not two_steps:
            exchange_wait(*exchange_g(p))
            return
        for k, distance in near[:2]:
            hop(p, k, away(-distance), away(distance)).wait_recv()
        for k, distance in ((4, -3), (5, 3), (6, 4)):
            hop(p, k, away(distance), away(1)).wait_recv()
        for k, distance in near:
            hop(p, k, mez, away(distance)).wait_send()
        for k, chunk, target in far:
            hop(p, k, chunk, target).wait_send()

    for l in range(owned):
        render_back(l)
        head = jnp.concatenate([wb_out[l].astype(f32)] * 4, 0).astype(bf16)

        def second_grad(c):
            grad_two[l, c] = jnp.where(hid_two[l, c] > 0, dot_tn(raw_grad[l, c], head).astype(bf16), zero)

        def first_grad(c):
            return jnp.where(hid_one[l, c] > 0, dot_nt(grad_two[l, c], wb_mid[l]).astype(bf16), zero)

        second_grad(0)
        for c in range(chunks):
            if c + 1 < chunks:
                second_grad(c + 1)
            term = dot(one_t[l, c], grad_two[l, c])
            acc[...] = term if c == 0 else acc[...] + term
        send_part(2 * l)
        if l > 0:
            sum_part(2 * l - 2)
            gather_near(2 * l - 2)
        now = first_grad(0)
        for c in range(chunks):
            later = first_grad(c + 1) if c + 1 < chunks else None
            term = dot(feat_t[l, c], now)
            acc[...] = term if c == 0 else acc[...] + term
            now = later
        send_part(2 * l + 1)

    sum_part(1)
    gather_near(1)

    half = hid_two.shape[3] // 2
    sums = []
    for l in range(owned):
        for c in range(chunks):
            term = dot(raw_grad[l, c], hid_two[l, c])
            acc_out[...] = term if c == 0 else acc_out[...] + term
        summed = untall(acc_out[...])[:4]
        sums += [summed[:, :half], summed[:, half:]]
    out_send[...] = jnp.concatenate(sums, 0).astype(bf16)
    exchange_o = (m, mez, "replica", lambda z: out_send, out_recv, sem_go.at[0], sem_go.at[1])
    exchange_start(*exchange_o)
    out_recv[mez] = out_send[...]

    sum_part(2)
    gather_near(2)
    gather_far(0)
    gather_far(1)
    sum_part(last)
    gather_near(last)
    gather_far(2)
    for exchange in (exchange_a, exchange_b, exchange_c):
        exchange_wait(*exchange, ("send",))
    exchange_wait(*exchange_o)
    total = out_recv[0].astype(f32)
    for k in range(1, m):
        total = total + out_recv[k].astype(f32)
    for l in range(owned):
        grad_out_ref[l] = jnp.concatenate([total[8 * l : 8 * l + 4], total[8 * l + 4 : 8 * l + 8]], 1)
    for p in range(2 * owned):
        gather_wait(p)


def finish_kernel(colour, grads, grad_out, colour_ref, grad_in_ref, grad_mid_ref, grad_out_ref):
    colour_ref[...] = colour[...]
    grad_out_ref[...] = grad_out[...]
    for l in range(grad_in_ref.shape[0]):
        grad_mid_ref[l] = grads[2 * l].astype(f32)
        grad_in_ref[l] = grads[2 * l + 1].astype(f32)


def on_device(positions, spacing, targets, seg_region, seg_rank, frequencies, w_in, w_mid, w_out):
    n, m = lax.axis_size("region"), lax.axis_size("replica")
    rays, segs = seg_rank.shape
    seg_len = positions.shape[2] // segs
    owned, enc, hid = w_in.shape
    cap = 3 * rays * segs // (owned * n)
    slots, chunk = n * cap, 2 * n * cap
    chunks = seg_len // 2
    groups = n * ROW // LANES
    deep = hid // m
    half = w_out.shape[2] // 2
    vmem = pltpu.VMEM
    semaphores = pltpu.SemaphoreType.DMA
    colour, grads, grad_out = pl.pallas_call(
        functools.partial(step_kernel, n, m, cap, segs, seg_len),
        out_shape=(
            jax.ShapeDtypeStruct((3, rays), f32),
            jax.ShapeDtypeStruct((2 * owned, m, deep, hid), bf16),
            jax.ShapeDtypeStruct(w_out.shape, f32),
        ),
        in_specs=[pl.BlockSpec(memory_space=vmem)] * 7 + [pl.BlockSpec(memory_space=pl.ANY)] * 2,
        out_specs=[pl.BlockSpec(memory_space=vmem)] * 3,
        scratch_shapes=[
            vmem((n, ROW, LANES), f32),
            vmem((n, ROW, LANES), f32),
            vmem((groups, 8, LANES), f32),
            vmem((n, 8, LANES), f32),
            vmem((n, 8, LANES), f32),
            vmem((n, 8, LANES), f32),
            vmem((owned, chunks, chunk, enc), bf16),
            vmem((owned, chunks, chunk, hid), bf16),
            vmem((owned, chunks, chunk, hid), bf16),
            vmem((owned, chunks, 8, chunk), f32),
            vmem((owned, seg_len, 8, slots), f32),
            vmem((owned, seg_len, 8, slots), f32),
            vmem((owned, seg_len, slots), f32),
            vmem((owned, chunks, 32, chunk), bf16),
            vmem((owned, chunks, chunk, hid), bf16),
            vmem((owned, chunks, enc, chunk), bf16),
            vmem((owned, chunks, hid, chunk), bf16),
            vmem((slots, n * ROW), bf16),
            vmem((chunks, 2 * LANES, enc), bf16),
            vmem((chunks, LANES, enc), bf16),
            vmem((owned, slots, 2 * LANES), bf16),
            vmem((owned, enc, hid), f32),
            vmem((owned, hid, hid), f32),
            vmem((owned, enc, hid), bf16),
            vmem((owned, hid, hid), bf16),
            vmem((owned, 8, hid), bf16),
            vmem((owned, hid, LANES), bf16),
            vmem((hid, hid), f32),
            vmem((32, hid), f32),
            vmem((2 * owned, m, deep, hid), bf16),
            vmem((2 * owned, m, deep, hid), bf16),
            vmem((8 * owned, half), bf16),
            vmem((m, 8 * owned, half), bf16),
            semaphores((2,)),
            semaphores((2, n)),
            semaphores((2, n)),
            semaphores((2, n)),
            semaphores((2 * owned, 2, m)),
            semaphores((2 * owned, 2, m)),
            semaphores((2, m)),
        ],
        compiler_params=pltpu.CompilerParams(
            collective_id=0, has_side_effects=True, vmem_limit_bytes=56 * 2**20
        ),
        name="radiance_step",
    )(
        positions, spacing, targets, seg_region.transpose(1, 2, 0), seg_rank.T, frequencies, w_out, w_in, w_mid
    )
    return pl.pallas_call(
        finish_kernel,
        out_shape=(
            jax.ShapeDtypeStruct(colour.shape, f32),
            jax.ShapeDtypeStruct(w_in.shape, f32),
            jax.ShapeDtypeStruct(w_mid.shape, f32),
            jax.ShapeDtypeStruct(w_out.shape, f32),
        ),
        in_specs=[pl.BlockSpec(memory_space=vmem)] * 3,
        out_specs=[pl.BlockSpec(memory_space=vmem)] * 4,
        name="widen",
    )(colour, grads.reshape(2 * owned, hid, hid), grad_out)


def solution(mesh):
    in_specs = (
        P(None, ("region", "replica"), None),
        P(("region", "replica"), None),
        P(None, ("region", "replica")),
        P(("region", "replica"), None, None),
        P(("region", "replica"), None),
        P(),
        P("region", None, None),
        P("region", None, None),
        P("region", None, None),
    )
    out_specs = (
        P(None, ("region", "replica")),
        P("region", None, None),
        P("region", None, None),
        P("region", None, None),
    )
    return jax.shard_map(
        on_device, mesh=mesh, in_specs=in_specs, out_specs=out_specs, check_vma=False
    )
```

```python
import functools

import jax
import jax.numpy as jnp
from jax import lax
from jax.experimental import pallas as pl
from jax.experimental.pallas import tpu as pltpu
from jax.sharding import PartitionSpec as P

MESH = pl.DeviceIdType.MESH
f32, bf16 = jnp.float32, jnp.bfloat16
LANES = 128
ROW = 16
loss_scale = 16.0

SIN_HALF = (4.442882919048677, -7.308245676836255, 3.606354025126868, -0.8461104138552027, 0.10982204430121903)
COS_HALF = (1.4142134959439656, -6.978850908781684, 5.739459581977078, -1.8835528214703008, 0.31067786282805515)


def iota(shape, dim):
    return lax.broadcasted_iota(jnp.int32, shape, dim)


def dot(a, b):
    return jnp.dot(a, b, preferred_element_type=f32)


def dot_nt(a, b):
    return lax.dot_general(a, b, (((1,), (1,)), ((), ())), preferred_element_type=f32)


def dot_tn(a, b):
    return lax.dot_general(a, b, (((0,), (0,)), ((), ())), preferred_element_type=f32)


def split(x):
    high = x.astype(bf16).astype(f32)
    rest = x - high
    middle = rest.astype(bf16).astype(f32)
    return high, middle, rest - middle


def wide(x):
    return jnp.concatenate(split(x), 1).astype(bf16)


def tall(x):
    return jnp.concatenate((*split(x), jnp.zeros_like(x)), 0).astype(bf16)


def unwide(x):
    w = x.shape[1] // 3
    return x[:, :w] + x[:, w : 2 * w] + x[:, 2 * w :]


def untall(x):
    w = x.shape[0] // 4
    return x[:w] + x[w : 2 * w] + x[2 * w : 3 * w]


def polynomial(coefficients, z):
    value = jnp.full_like(z, coefficients[-1])
    for coefficient in coefficients[-2::-1]:
        value = value * z + coefficient
    return value


def sin_cos_turns(turns):
    rest = turns - jnp.round(turns)
    square = rest * rest
    s = polynomial(SIN_HALF, square) * rest
    c = polynomial(COS_HALF, square)
    return s * c, 1.0 - s * s


def column_from_row(eye, row):
    return jnp.sum(jnp.where(eye, jnp.broadcast_to(row, eye.shape), 0.0), axis=1, keepdims=True)


def on_lanes(x, width=LANES):
    return jnp.concatenate([x, jnp.zeros((x.shape[0], width - x.shape[1]), x.dtype)], 1)


def exchange_start(count, me, axis, source_of, target, send, recv):
    def start(k, carry):
        peer = lax.rem(me + k, count)
        pltpu.make_async_remote_copy(
            src_ref=source_of(peer),
            dst_ref=target.at[me],
            send_sem=send.at[k],
            recv_sem=recv.at[k],
            device_id={axis: peer},
            device_id_type=MESH,
        ).start()
        return carry

    lax.fori_loop(1, count, start, 0)


def exchange_wait(count, me, axis, source_of, target, send, recv, sides=("recv", "send")):
    def wait(k, carry):
        peer = lax.rem(me + k, count)
        origin = lax.rem(me + count - k, count)
        copy = pltpu.make_async_remote_copy(
            src_ref=source_of(peer),
            dst_ref=target.at[origin],
            send_sem=send.at[k],
            recv_sem=recv.at[k],
            device_id={axis: peer},
            device_id_type=MESH,
        )
        if "recv" in sides:
            copy.wait_recv()
        if "send" in sides:
            copy.wait_send()
        return carry

    lax.fori_loop(1, count, wait, 0)


def step_kernel(
    n, m, cap, segs, seg_len,
    pos_ref, gap_ref, tgt_ref, reg_ref, rank_ref, freq_ref, w_out_ref, w_in_hbm, w_mid_hbm,
    colour_ref, grads_ref, grad_out_ref,
    send_a, recv_a, send_b, recv_b, send_c, recv_c,
    feat, hid_one, hid_two, raw, shade, alpha, gaps, raw_grad, grad_two, feat_t, one_t,
    place, phase_table, slots_x, w_in, w_mid, wb_in, wb_mid, wb_out, wb_out_t,
    acc, acc_out, part, part_recv, out_send, out_recv,
    sem_w, sem_a, sem_b, sem_c, sem_rs, sem_ag, sem_go,
):
    me = lax.axis_index("region")
    mez = lax.axis_index("replica")
    owned = w_in.shape[0]
    rays = pos_ref.shape[1]
    seg_dev = rays * segs
    slots = n * cap
    chunks = seg_len // 2
    per_tile = LANES // ROW
    half_lanes = LANES // 2

    barrier = pltpu.get_barrier_semaphore()

    def greet_region(k, carry):
        pl.semaphore_signal(
            barrier, inc=1, device_id={"region": lax.rem(me + k, n)}, device_id_type=MESH
        )
        return carry

    def greet_replica(k, carry):
        pl.semaphore_signal(
            barrier, inc=1, device_id={"replica": lax.rem(mez + k, m)}, device_id_type=MESH
        )
        return carry

    lax.fori_loop(1, n, greet_region, 0)
    lax.fori_loop(1, m, greet_replica, 0)
    load_in = pltpu.make_async_copy(w_in_hbm, w_in, sem_w.at[0])
    load_mid = pltpu.make_async_copy(w_mid_hbm, w_mid, sem_w.at[1])
    load_in.start()
    load_mid.start()

    eye = iota((rays, rays), 0) == iota((rays, rays), 1)
    region_col = jnp.concatenate([column_from_row(eye, reg_ref[s].astype(f32)) for s in range(segs)], 0)
    lane = iota((seg_dev, LANES), 1)
    onehot = jnp.where(region_col == lane.astype(f32), 1.0, 0.0)
    before = jnp.where(iota((seg_dev, seg_dev), 0) > iota((seg_dev, seg_dev), 1), 1.0, 0.0)
    earlier = dot(before.astype(bf16), onehot.astype(bf16))
    order_col = jnp.sum(earlier * onehot, axis=1, keepdims=True)
    owner_col = jnp.floor((region_col + 0.5) * (1.0 / owned))
    local_col = region_col - owned * owner_col
    keys = jnp.where(lane == 0, owner_col * ROW + order_col, jnp.where(lane == 1, owner_col, 0.0)).T
    slot_row, owner_row = keys[0:1, :], keys[1:2, :]

    pieces = []
    lane_s = iota((rays, LANES), 1) & (half_lanes - 1)
    for s in range(segs):
        packed = jnp.zeros((rays, LANES), f32)
        for d in range(4):
            source = on_lanes(pos_ref[d] if d < 3 else gap_ref[...].astype(f32))
            shift = seg_len * (d - s)
            moved = pltpu.roll(source, shift % LANES, 1)
            packed = jnp.where((lane_s >= seg_len * d) & (lane_s < seg_len * (d + 1)), moved, packed)
        pieces.append(packed[:, :])
    packed = jnp.concatenate(pieces, 0)
    packed = jnp.where(lane < half_lanes, packed, pltpu.roll(packed, half_lanes, 1))
    own_half = (lane >= half_lanes).astype(f32) == local_col
    packed = wide(jnp.where(own_half, packed, 0.0))
    scatter = jnp.where(iota((n * ROW, seg_dev), 0).astype(f32) == slot_row, 1.0, 0.0).astype(bf16)
    send_a[...] = unwide(dot(scatter, packed)).reshape(send_a.shape)

    pl.semaphore_wait(barrier, n - 1 + m - 1)
    exchange_a = (n, me, "region", lambda p: send_a.at[p], recv_a, sem_a.at[0], sem_a.at[1])
    exchange_start(*exchange_a)
    recv_a[me] = send_a[me]

    slot_id = iota((slots, 1), 0).astype(f32)
    peer_id = jnp.floor((slot_id + 0.5) * (1.0 / cap))
    spot = slot_id + (ROW - cap) * peer_id
    place[...] = jnp.where(iota((slots, n * ROW), 1).astype(f32) == spot, 1.0, 0.0).astype(bf16)
    freq_high, freq_middle, freq_low = split(freq_ref[...])
    width = freq_ref.shape[1]

    def spread(values):
        return jnp.concatenate([jnp.broadcast_to(values[d : d + 1], (seg_len, width)) for d in range(3)], 0)

    rest16 = jnp.zeros((seg_len, width), f32)
    rest32 = jnp.zeros((2 * seg_len, width), f32)
    table_hi = jnp.concatenate(
        [spread(freq_high), spread(freq_high), rest32, spread(freq_high), rest16, spread(freq_middle), rest16], 0
    )
    table_lo = jnp.concatenate([spread(freq_low), spread(freq_middle), rest32], 0)
    for i in range(seg_len):
        cols = slice((i % 2) * width, (i % 2 + 1) * width)
        mine = (iota(table_hi.shape, 0) & (seg_len - 1)) == i
        phase_table[i // 2, : 2 * LANES, cols] = jnp.where(mine, table_hi, 0.0).astype(bf16)
        mine = (iota(table_lo.shape, 0) & (seg_len - 1)) == i
        phase_table[i // 2, 2 * LANES :, cols] = jnp.where(mine, table_lo, 0.0).astype(bf16)
    load_in.wait()
    load_mid.wait()
    for l in range(owned):
        wb_in[l] = w_in[l].astype(bf16)
        wb_mid[l] = w_mid[l].astype(bf16)
        out_rows = jnp.concatenate([w_out_ref[l], jnp.zeros((LANES - 4, w_out_ref.shape[2]), f32)], 0)
        wb_out[l] = out_rows[:8].astype(bf16)
        wb_out_t[l] = out_rows.T.astype(bf16)

    exchange_wait(*exchange_a, ("recv",))

    high, middle, low = split(recv_a[...].reshape(n * ROW, LANES))
    lane_r = iota(high.shape, 1)
    coords = 3 * seg_len
    high_turned = pltpu.roll(high, half_lanes, 1)
    pick_gap = jnp.where(
        iota((seg_len, 3 * LANES), 1) == iota((seg_len, 3 * LANES), 0) + LANES + coords, 1.0, 0.0
    ).astype(bf16)
    for l in range(owned):
        own, other = (high, high_turned) if l == 0 else (high_turned, high)
        tail = low if l == 0 else pltpu.roll(low, half_lanes, 1)
        first = jnp.where(lane_r < coords, own, pltpu.roll(middle, coords + l * half_lanes, 1))
        second = jnp.where(lane_r < coords, tail, jnp.where(lane_r < half_lanes, own, other))
        slots_x[l] = dot(place[...], jnp.concatenate([first, second, first], 1).astype(bf16)).astype(bf16)
        gaps[l] = dot_nt(pick_gap, slots_x[l])

    def phases(l, c):
        return dot(slots_x[l], phase_table[c])

    def encode(l, c, turns):
        sines, cosines = sin_cos_turns(turns)
        for j in range(2):
            cols = slice(j * width, (j + 1) * width)
            feat[l, c, j * slots : (j + 1) * slots, :] = jnp.concatenate(
                [sines[:, cols], cosines[:, cols]], 1
            ).astype(bf16)

    def render(l):
        depth = jnp.zeros((8, slots), f32)
        clear = jnp.ones((8, slots), f32)
        colour = jnp.zeros((8, slots), f32)
        for i in range(seg_len):
            value = raw[l, i // 2][:, (i % 2) * slots : (i % 2 + 1) * slots]
            density = jnp.broadcast_to(value[0:1], value.shape)
            density = jnp.maximum(density, 0.0) + jnp.log1p(jnp.exp(-jnp.abs(density)))
            emitted = 1.0 / (1.0 + jnp.exp(-value))
            depth = depth + density * gaps[l][i : i + 1]
            after = jnp.exp(-depth)
            colour = colour + (clear - after) * emitted
            clear = after
            shade[l, i] = emitted
            alpha[l, i] = after
        return jnp.where(sub == 0, clear, colour)[:4]

    sub = iota((8, slots), 0)
    zero = jnp.zeros((), bf16)
    steps = [(l, c) for c in range(chunks) for l in range(owned)]
    encode(*steps[0], phases(*steps[0]))
    rendered = []
    for at, (l, c) in enumerate(steps):
        ahead = steps[at + 1] if at + 1 < len(steps) else None
        if ahead:
            turns = phases(*ahead)
        one = jnp.maximum(dot(feat[l, c], wb_in[l]).astype(bf16), zero)
        hid_one[l, c] = one
        if ahead:
            encode(*ahead, turns)
        two = jnp.maximum(dot(one, wb_mid[l]).astype(bf16), zero)
        hid_two[l, c] = two
        raw[l, c] = dot(two, wb_out_t[l]).T[:8]
        if c == chunks - 1:
            rendered.append(render(l))
    returned = untall(dot(tall(jnp.concatenate(rendered, 0)), place[...]))
    for q in range(send_b.shape[0]):
        send_b[q] = returned[:, q * LANES : (q + 1) * LANES]

    exchange_b = (n, me, "region", lambda p: send_b.at[p // per_tile], recv_b, sem_b.at[0], sem_b.at[1])
    exchange_start(*exchange_b)
    recv_b[me] = send_b[me // per_tile]

    unit_mask = ((lane & (ROW - 1)).astype(f32) == order_col) & own_half
    channel = (lane // ROW) & 3
    owner_mask = jnp.where(iota((seg_dev, n), 1).astype(f32) == owner_col, 1.0, 0.0).astype(bf16)
    owner_turned = jnp.where(iota((n, seg_dev), 0).astype(f32) == owner_row, 1.0, 0.0).astype(bf16)
    rank = [column_from_row(eye, rank_ref[s : s + 1, :].astype(f32)) for s in range(segs)]
    earlier_than = [[rank[t] < rank[s] for t in range(segs)] for s in range(segs)]
    target = [column_from_row(eye, tgt_ref[c : c + 1, :]) for c in range(3)]
    shift_home = lax.rem(me, per_tile) * ROW

    for l in range(owned):
        for c in range(chunks):
            one_t[l, c] = hid_one[l, c].T

    exchange_wait(*exchange_b, ("recv",))

    lane_n = iota((n, LANES), 1)
    mine = jnp.zeros((n, LANES), f32)
    for ch in range(8):
        moved = pltpu.roll(recv_b[:, ch, :], lax.rem(ch * ROW - shift_home + LANES, LANES), 1)
        mine = jnp.where((lane_n >= ch * ROW) & (lane_n < (ch + 1) * ROW), moved, mine)
    found = jnp.where(unit_mask, unwide(dot(owner_mask, wide(mine))), 0.0)
    columns = [jnp.sum(jnp.where(channel == ch, found, 0.0), axis=1, keepdims=True) for ch in range(4)]
    by_seg = [[col[s * rays : (s + 1) * rays] for s in range(segs)] for col in columns]
    trans, colours = by_seg[0], by_seg[1:]

    def front(s, skip):
        product = jnp.ones((rays, 1), f32)
        for t in range(segs):
            if t not in skip:
                product = product * jnp.where(earlier_than[s][t], trans[t], 1.0)
        return product

    prefix = [front(s, (s,)) for s in range(segs)]
    pulled = []
    for c in range(3):
        total = colours[c][0] * prefix[0]
        for s in range(1, segs):
            total = total + colours[c][s] * prefix[s]
        colour_ref[c : c + 1, :] = jnp.sum(
            jnp.where(eye, jnp.broadcast_to(total, eye.shape), 0.0), axis=0, keepdims=True
        )
        pulled.append((2.0 * loss_scale) * (total - target[c]))
    weight = [
        pulled[0] * colours[0][s] + pulled[1] * colours[1][s] + pulled[2] * colours[2][s] for s in range(segs)
    ]
    back = [[], [], [], []]
    for t in range(segs):
        total = jnp.zeros((rays, 1), f32)
        for s in range(segs):
            if s != t:
                total = total + jnp.where(earlier_than[s][t], weight[s] * front(s, (s, t)), 0.0)
        back[0].append(total)
        for c in range(3):
            back[c + 1].append(pulled[c] * prefix[t])
    spread_back = jnp.zeros((seg_dev, LANES), f32)
    for ch in range(4):
        spread_back = jnp.where(channel == ch, jnp.concatenate(back[ch], 0), spread_back)
    spread_back = jnp.where(unit_mask, spread_back, 0.0)
    homeward = unwide(dot(owner_turned, wide(spread_back)))
    for ch in range(8):
        moved = pltpu.roll(homeward, lax.rem(shift_home - ch * ROW + LANES, LANES), 1)
        send_c[:, ch, :] = jnp.where((lane_n >= shift_home) & (lane_n < shift_home + ROW), moved, 0.0)

    exchange_c = (n, me, "region", lambda p: send_c.at[p], recv_c, sem_c.at[0], sem_c.at[1])
    exchange_start(*exchange_c)
    recv_c[me] = send_c[me]
    for l in range(owned):
        for c in range(chunks):
            feat_t[l, c] = feat[l, c].T
    exchange_wait(*exchange_c, ("recv",))

    groups = []
    for q in range(send_b.shape[0]):
        total = recv_c[q * per_tile]
        for k in range(1, per_tile):
            total = total + recv_c[q * per_tile + k]
        groups.append(total)
    cotangent = untall(dot_nt(tall(jnp.concatenate(groups, 1)), place[...]))

    def render_back(l):
        pull = cotangent if l == 0 else pltpu.roll(cotangent, 4, 0)
        later = pull[0:1] * alpha[l, seg_len - 1][0:1]
        for i in range(seg_len - 1, -1, -1):
            emitted = shade[l, i]
            after = alpha[l, i]
            ahead = alpha[l, i - 1] if i > 0 else jnp.ones_like(after)
            share = ahead - after
            lit = pull * emitted
            lit = jnp.sum(jnp.where((sub >= 1) & (sub <= 3), lit, 0.0), axis=0, keepdims=True)
            later = later + lit * share[0:1]
            density = (lit * ahead[0:1] - later) * gaps[l][i : i + 1] * emitted[0:1]
            tint = pull * share * emitted * (1.0 - emitted)
            values = jnp.where(sub == 0, density, jnp.where(sub <= 3, tint, 0.0))
            raw_grad[l, i // 2, :, (i % 2) * slots : (i % 2 + 1) * slots] = tall(values)

    def exchange_r(p):
        return (m, mez, "replica", lambda z: part.at[p, z], part_recv.at[p], sem_rs.at[p, 0], sem_rs.at[p, 1])

    def exchange_g(p):
        return (m, mez, "replica", lambda z: grads_ref.at[p, mez], grads_ref.at[p], sem_ag.at[p, 0], sem_ag.at[p, 1])

    def send_part(p):
        part[p] = acc[...].astype(bf16).reshape(part.shape[1:])
        exchange_start(*exchange_r(p))

    def sum_part(p):
        part_recv[p, mez] = part[p, mez]
        exchange_wait(*exchange_r(p))
        total = part_recv[p, 0].astype(f32)
        for k in range(1, m):
            total = total + part_recv[p, k].astype(f32)
        grads_ref[p, mez] = total.astype(bf16)

    two_steps = m == 8
    last = 2 * owned - 1

    def hop(p, k, chunk, target):
        return pltpu.make_async_remote_copy(
            src_ref=grads_ref.at[p, chunk],
            dst_ref=grads_ref.at[p, chunk],
            send_sem=sem_ag.at[p, 0, k],
            recv_sem=sem_ag.at[p, 1, k],
            device_id={"replica": target},
            device_id_type=MESH,
        )

    def away(distance):
        return lax.rem(mez + distance + m, m)

    side = 2 - 4 * lax.rem(mez, 2)
    near = ((0, 1), (1, -1), (2, 2), (3, -2))
    far = ((4, away(-2), away(1)), (5, away(2), away(-1)), (6, away(-side), away(side)))

    def gather_near(p):
        if p == last or not two_steps:
            exchange_start(*exchange_g(p))
            return
        for k, distance in near:
            hop(p, k, mez, away(distance)).start()

    def gather_far(p):
        if p == last or not two_steps:
            return
        for k, distance in near[2:]:
            hop(p, k, away(-distance), away(distance)).wait_recv()
        for k, chunk, target in far:
            hop(p, k, chunk, target).start()

    def gather_wait(p):
        if p == last or not two_steps:
            exchange_wait(*exchange_g(p))
            return
        for k, distance in near[:2]:
            hop(p, k, away(-distance), away(distance)).wait_recv()
        for k, distance in ((4, -3), (5, 3), (6, 4)):
            hop(p, k, away(distance), away(1)).wait_recv()
        for k, distance in near:
            hop(p, k, mez, away(distance)).wait_send()
        for k, chunk, target in far:
            hop(p, k, chunk, target).wait_send()

    for l in range(owned):
        render_back(l)
        head = jnp.concatenate([wb_out[l].astype(f32)] * 4, 0).astype(bf16)

        def second_grad(c):
            grad_two[l, c] = jnp.where(hid_two[l, c] > 0, dot_tn(raw_grad[l, c], head).astype(bf16), zero)

        def first_grad(c):
            return jnp.where(hid_one[l, c] > 0, dot_nt(grad_two[l, c], wb_mid[l]).astype(bf16), zero)

        second_grad(0)
        for c in range(chunks):
            if c + 1 < chunks:
                second_grad(c + 1)
            term = dot(one_t[l, c], grad_two[l, c])
            acc[...] = term if c == 0 else acc[...] + term
        send_part(2 * l)
        if l > 0:
            sum_part(2 * l - 2)
            gather_near(2 * l - 2)
        now = first_grad(0)
        for c in range(chunks):
            later = first_grad(c + 1) if c + 1 < chunks else None
            term = dot(feat_t[l, c], now)
            acc[...] = term if c == 0 else acc[...] + term
            now = later
        send_part(2 * l + 1)

    sum_part(1)
    gather_near(1)

    half = hid_two.shape[3] // 2
    sums = []
    for l in range(owned):
        for c in range(chunks):
            term = dot(raw_grad[l, c], hid_two[l, c])
            acc_out[...] = term if c == 0 else acc_out[...] + term
        summed = untall(acc_out[...])[:4]
        sums += [summed[:, :half], summed[:, half:]]
    out_send[...] = jnp.concatenate(sums, 0).astype(bf16)
    exchange_o = (m, mez, "replica", lambda z: out_send, out_recv, sem_go.at[0], sem_go.at[1])
    exchange_start(*exchange_o)
    out_recv[mez] = out_send[...]

    sum_part(2)
    gather_near(2)
    gather_far(0)
    gather_far(1)
    sum_part(last)
    gather_near(last)
    gather_far(2)
    for exchange in (exchange_a, exchange_b, exchange_c):
        exchange_wait(*exchange, ("send",))
    exchange_wait(*exchange_o)
    total = out_recv[0].astype(f32)
    for k in range(1, m):
        total = total + out_recv[k].astype(f32)
    for l in range(owned):
        grad_out_ref[l] = jnp.concatenate([total[8 * l : 8 * l + 4], total[8 * l + 4 : 8 * l + 8]], 1)
    for p in range(2 * owned):
        gather_wait(p)


def finish_kernel(colour, grads, grad_out, colour_ref, grad_in_ref, grad_mid_ref, grad_out_ref):
    colour_ref[...] = colour[...]
    grad_out_ref[...] = grad_out[...]
    for l in range(grad_in_ref.shape[0]):
        grad_mid_ref[l] = grads[2 * l].astype(f32)
        grad_in_ref[l] = grads[2 * l + 1].astype(f32)


def on_device(positions, spacing, targets, seg_region, seg_rank, frequencies, w_in, w_mid, w_out):
    n, m = lax.axis_size("region"), lax.axis_size("replica")
    rays, segs = seg_rank.shape
    seg_len = positions.shape[2] // segs
    owned, enc, hid = w_in.shape
    cap = 3 * rays * segs // (owned * n)
    slots, chunk = n * cap, 2 * n * cap
    chunks = seg_len // 2
    groups = n * ROW // LANES
    deep = hid // m
    half = w_out.shape[2] // 2
    vmem = pltpu.VMEM
    semaphores = pltpu.SemaphoreType.DMA
    colour, grads, grad_out = pl.pallas_call(
        functools.partial(step_kernel, n, m, cap, segs, seg_len),
        out_shape=(
            jax.ShapeDtypeStruct((3, rays), f32),
            jax.ShapeDtypeStruct((2 * owned, m, deep, hid), bf16),
            jax.ShapeDtypeStruct(w_out.shape, f32),
        ),
        in_specs=[pl.BlockSpec(memory_space=vmem)] * 7 + [pl.BlockSpec(memory_space=pl.ANY)] * 2,
        out_specs=[pl.BlockSpec(memory_space=vmem)] * 3,
        scratch_shapes=[
            vmem((n, ROW, LANES), f32),
            vmem((n, ROW, LANES), f32),
            vmem((groups, 8, LANES), f32),
            vmem((n, 8, LANES), f32),
            vmem((n, 8, LANES), f32),
            vmem((n, 8, LANES), f32),
            vmem((owned, chunks, chunk, enc), bf16),
            vmem((owned, chunks, chunk, hid), bf16),
            vmem((owned, chunks, chunk, hid), bf16),
            vmem((owned, chunks, 8, chunk), f32),
            vmem((owned, seg_len, 8, slots), f32),
            vmem((owned, seg_len, 8, slots), f32),
            vmem((owned, seg_len, slots), f32),
            vmem((owned, chunks, 32, chunk), bf16),
            vmem((owned, chunks, chunk, hid), bf16),
            vmem((owned, chunks, enc, chunk), bf16),
            vmem((owned, chunks, hid, chunk), bf16),
            vmem((slots, n * ROW), bf16),
            vmem((chunks, 3 * LANES, enc), bf16),
            vmem((owned, slots, 3 * LANES), bf16),
            vmem((owned, enc, hid), f32),
            vmem((owned, hid, hid), f32),
            vmem((owned, enc, hid), bf16),
            vmem((owned, hid, hid), bf16),
            vmem((owned, 8, hid), bf16),
            vmem((owned, hid, LANES), bf16),
            vmem((hid, hid), f32),
            vmem((32, hid), f32),
            vmem((2 * owned, m, deep, hid), bf16),
            vmem((2 * owned, m, deep, hid), bf16),
            vmem((8 * owned, half), bf16),
            vmem((m, 8 * owned, half), bf16),
            semaphores((2,)),
            semaphores((2, n)),
            semaphores((2, n)),
            semaphores((2, n)),
            semaphores((2 * owned, 2, m)),
            semaphores((2 * owned, 2, m)),
            semaphores((2, m)),
        ],
        compiler_params=pltpu.CompilerParams(
            collective_id=0, has_side_effects=True, vmem_limit_bytes=56 * 2**20
        ),
        name="radiance_step",
    )(
        positions, spacing, targets, seg_region.transpose(1, 2, 0), seg_rank.T, frequencies, w_out, w_in, w_mid
    )
    return pl.pallas_call(
        finish_kernel,
        out_shape=(
            jax.ShapeDtypeStruct(colour.shape, f32),
            jax.ShapeDtypeStruct(w_in.shape, f32),
            jax.ShapeDtypeStruct(w_mid.shape, f32),
            jax.ShapeDtypeStruct(w_out.shape, f32),
        ),
        in_specs=[pl.BlockSpec(memory_space=vmem)] * 3,
        out_specs=[pl.BlockSpec(memory_space=vmem)] * 4,
        name="widen",
    )(colour, grads.reshape(2 * owned, hid, hid), grad_out)


def solution(mesh):
    in_specs = (
        P(None, ("region", "replica"), None),
        P(("region", "replica"), None),
        P(None, ("region", "replica")),
        P(("region", "replica"), None, None),
        P(("region", "replica"), None),
        P(),
        P("region", None, None),
        P("region", None, None),
        P("region", None, None),
    )
    out_specs = (
        P(None, ("region", "replica")),
        P("region", None, None),
        P("region", None, None),
        P("region", None, None),
    )
    return jax.shard_map(
        on_device, mesh=mesh, in_specs=in_specs, out_specs=out_specs, check_vma=False
    )
```
